32 devices in a mesh: tm: 8 (over z, y), table: 4 (over x, core).
Axes of the slice: x: 2, y: 2, z: 4, core: 2. Of those that a mesh axis runs over, the one named last changes fastest.
Arguments:
- item_owner: int32 [8, 6144, 1], P('table', 'tm'), may hold values from 0 to 31; in each aligned block of 768 rows (0 to 767, 768 to 1535, ..., all dimensions but the last counted through in order) at most 48 rows name the same one
- item_row: int32 [8, 6144], P('table', 'tm'), may hold values from 0 to 4095
- history_len: int32 [8], P('table'), may hold values from 1536 to 6144, as said below
- event_gap: float32 [8, 6144], P('table', 'tm'), may hold values from 0 to 18432, as said below
- item_table: bfloat16 [131072, 512], P(('tm', 'table')), may hold values from -6 to 6
- norm_gain: float32 [512], replicated, may hold values from 0.1 to 1.9
- in_weight: bfloat16 [512, 2192], replicated, may hold values from -0.25 to 0.25
- conv_weight: float32 [4, 1152], replicated, may hold values from -3 to 3
- conv_bias: float32 [1152], replicated, may hold values from -3 to 3
- dt_bias: float32 [16], replicated, may hold values from -1 to 1
- decay_rate: float32 [16], replicated, may hold values from 0 to 16, as said below
- out_gain: float32 [1024], replicated, may hold values from 0.1 to 1.9
- emitted_projection: bfloat16 [1024, 512], replicated, may hold values from -0.1875 to 0.1875
Outputs:
- layer_out: bfloat16 [8, 6144, 512], P('table', 'tm')
The draws below stay inside these ranges and needn't reach their ends.
Inputs may be any that keep to these rules, and one draw needn't show every extreme that they name: `item_owner`: in every user's 768 events held by one device no owner is named more than 48 times, a bound that some block reaches. `history_len`: some user has all 6144 events and some user 6144 // 4. `event_gap`: Positive. `decay_rate`: Positive.
All inputs are finite; a program needn't handle non-finite values.
Results may differ from the reference program's by a relative error of at most 0.01.
Values may be sent and summed in bfloat16 or wider, within the bound.
A program may use at most 192 MiB of HBM per device.

```python
import math
import jax
import jax.numpy as jnp
import numpy as np
from jax import lax

D = 512
HEADS = 16
HEAD_DIM = 64
STATE = 64
BLOCK = 256
ITEMS_DEV = 4096
EV = 768
DI = 1024
CONVW = 1152
PROJ = 2192
CUSTOMER_COUNT = 8
PAST_ACTIONS = 6144
CAP = 48
ITEMS = 131072
DEVICES = 32


def draw_history_len(key, part):
    first_key, auxiliary_seed, third_key = jax.random.split(key, 3)
    lengths = jax.random.randint(first_key, (CUSTOMER_COUNT,), PAST_ACTIONS // 4, PAST_ACTIONS + 1)
    longest = jax.random.randint(auxiliary_seed, (), 0, CUSTOMER_COUNT)
    shortest = (longest + jax.random.randint(third_key, (), 1, CUSTOMER_COUNT)) % CUSTOMER_COUNT
    user_index = jnp.arange(CUSTOMER_COUNT)
    lengths = jnp.where(user_index == longest, PAST_ACTIONS, lengths)
    lengths = jnp.where(user_index == shortest, PAST_ACTIONS // 4, lengths)
    return lengths.astype(jnp.int32)


def draw_event_gap(key, part):
    first_key, auxiliary_seed, third_key = jax.random.split(key, 3)
    typical_scenario = jnp.exp(jax.random.uniform(first_key, (CUSTOMER_COUNT, PAST_ACTIONS), jnp.float32, math.log(0.5), math.log(2.0)))
    action_cluster = jax.random.randint(auxiliary_seed, (CUSTOMER_COUNT, PAST_ACTIONS), 0, PAST_ACTIONS) < 4
    extended_record = PAST_ACTIONS * jax.random.uniform(third_key, (CUSTOMER_COUNT, PAST_ACTIONS), jnp.float32, 1.5, 3.0)
    return jnp.where(action_cluster, extended_record, typical_scenario).astype(jnp.float32)


def draw_decay_rate(key, part):
    first_key, auxiliary_seed, third_key = jax.random.split(key, 3)
    slow_share = 5
    slow_heads = jax.random.randint(first_key, (HEADS,), 0, 10) < slow_share
    slow_rate = jnp.exp(jax.random.uniform(auxiliary_seed, (HEADS,), jnp.float32, math.log(1.0 / (8 * PAST_ACTIONS)), math.log(1.0 / (2 * PAST_ACTIONS))))
    fast_rate = jnp.exp(jax.random.uniform(third_key, (HEADS,), jnp.float32, math.log(4.0 / BLOCK), math.log(16.0 / BLOCK)))
    return jnp.where(slow_heads, slow_rate, fast_rate).astype(jnp.float32)


def plant(entries, own_key, smallest, largest):
    longest = entries.shape.index(max(entries.shape))
    spots = []
    for shift in (0, 1):
        where = [jax.random.randint(jax.random.fold_in(own_key, axis), (), 0, length) for axis, length in enumerate(entries.shape)]
        where[longest] = (where[longest] + shift) % entries.shape[longest]
        spots.append(tuple(where))
    return entries.at[spots[0]].set(smallest).at[spots[1]].set(largest)


def levels(stream_key, shape, pieces, smallest, high):
    level = 1.0
    for position, parts in pieces:
        steps = jax.random.uniform(jax.random.fold_in(jax.random.fold_in(stream_key, 6), position), (parts,), jnp.float32, smallest / len(pieces), high / len(pieces))
        level = level * jnp.repeat(jnp.exp(steps), shape[position] // parts).reshape((-1,) + (1,) * (len(shape) - 1 - position))
    return level


def deal_out(key, own, number, rows, number_of, top, limit, skew):
    order = jax.random.permutation(key, number_of)
    crowded, usual = portions_of(number_of, rows * top, limit, skew, True), portions_of(number_of, rows * top, limit, skew, False)
    places = jnp.arange(number_of)

    def named(sizes, rotation):
        used = int((sizes > 0).sum())
        fixed = max(1, used // 4)
        passed = fixed + (places - fixed + rotation * (used - fixed)) % max(1, number_of - fixed)
        return jnp.zeros((number_of,), jnp.int32).at[order[jnp.where(places < fixed, places, passed)]].set(jnp.asarray(sizes, jnp.int32))

    sizes = jnp.where(number % 4 == 0, named(crowded, number // 4), named(usual, number - number // 4 - 1))
    mixed = jax.random.permutation(jax.random.fold_in(own, 3), number_of)
    giver, sink = mixed[0:number_of // 2 * 2:2], mixed[1:number_of // 2 * 2:2]
    room = jnp.minimum(sizes[giver] - 1, limit - sizes[sink]) // 2
    room = jnp.where((giver == order[0]) | (sink == order[0]) | (sizes[sink] == 0), 0, jnp.maximum(room, 0))
    passed = jax.random.randint(jax.random.fold_in(own, 4), (number_of // 2,), 0, 1 << 20) % (room + 1)
    sizes = sizes.at[giver].add(-passed).at[sink].add(passed)
    members = jnp.searchsorted(jnp.cumsum(sizes), jnp.arange(rows * top), side="right").astype(jnp.int32)
    listing = members.reshape(top, rows).T
    listing = listing[jax.random.permutation(jax.random.fold_in(own, 1), rows)]
    rotation = jax.random.randint(jax.random.fold_in(own, 2), (rows, 1), 0, top)
    return jnp.take_along_axis(listing, (jnp.arange(top)[None, :] + rotation) % top, axis=1)


def portions_of(amount, total, most, slope, full):
    weights = [(1 << 20) // math.isqrt(grade ** slope) + 1 for grade in range(1, amount + 1)]
    largest = most if full else min(most, max(-(-total // amount), total * weights[0] // sum(weights)))
    least = 1 if total - largest >= amount - 1 else 0
    holding, surplus = [largest] + [least] * (amount - 1), total - largest - least * (amount - 1)
    while surplus > 0:
        movable = [i for i in range(1, amount) if holding[i] < largest] or [i for i in range(1, amount) if holding[i] < most]
        pool, budget = sum([weights[i] for i in movable]), surplus
        for i in movable:
            addition = min(most - holding[i], max(1, budget * weights[i] // pool), surplus)
            holding[i] = holding[i] + addition
            surplus = surplus - addition
    return np.array(holding)


def scatter_about(own_key, extent, width, reach, pieces=(), held_as=jnp.bfloat16):
    level = levels(own_key, extent, pieces, -0.22, 0.18) if pieces else 1.0
    result = jax.random.normal(own_key, extent, jnp.float32) * width * level
    return jnp.minimum(jnp.maximum(result, -reach), reach).astype(held_as)


def setup_inputs(seed: int = 0) -> dict:
    splits = jax.random.split(jax.random.key(seed), 14)
    item_owner_keys = jax.random.split(jax.random.fold_in(splits[0], 1), CUSTOMER_COUNT * PAST_ACTIONS // EV)
    item_owner_turns = jax.random.permutation(jax.random.fold_in(splits[0], 3), CUSTOMER_COUNT * PAST_ACTIONS // EV)
    item_owner = jax.vmap(lambda own, number: deal_out(jax.random.fold_in(splits[0], 2), own, number, EV, DEVICES, 1, CAP, 1))(item_owner_keys, item_owner_turns).reshape((CUSTOMER_COUNT, PAST_ACTIONS, 1))
    item_row = plant(jax.random.randint(splits[1], (CUSTOMER_COUNT, PAST_ACTIONS), 0, ITEMS_DEV), jax.random.fold_in(splits[1], 1), 0, ITEMS_DEV - 1).astype(jnp.int32)
    history_len = draw_history_len(jax.random.fold_in(splits[13], 71), 0)
    event_gap = draw_event_gap(jax.random.fold_in(splits[13], 71), 0)
    item_table = scatter_about(splits[4], (ITEMS, D), 1.0, 6.0, ((0, 32),))
    norm_gain = jnp.clip(1.0 + 0.18 * jax.random.normal(splits[5], (D,), jnp.float32), 0.1, 1.9)
    in_weight = scatter_about(splits[6], (D, PROJ), D ** -0.5, 0.25)
    conv_weight = scatter_about(splits[7], (4, CONVW), 4 ** -0.5, 3.0, (), jnp.float32)
    conv_bias = scatter_about(splits[8], (CONVW,), 0.5, 3.0, (), jnp.float32)
    dt_bias = jnp.clip(jax.random.uniform(splits[9], (HEADS,), jnp.float32, -1.0, 1.0), -1.0, 1.0)
    decay_rate = draw_decay_rate(jax.random.fold_in(splits[13], 71), 0)
    out_gain = jnp.clip(1.0 + 0.18 * jax.random.normal(splits[11], (DI,), jnp.float32), 0.1, 1.9)
    emitted_projection = scatter_about(splits[12], (DI, D), DI ** -0.5, 0.1875)
    return {"item_owner": item_owner, "item_row": item_row, "history_len": history_len, "event_gap": event_gap, "item_table": item_table, "norm_gain": norm_gain, "in_weight": in_weight, "conv_weight": conv_weight, "conv_bias": conv_bias, "dt_bias": dt_bias, "decay_rate": decay_rate, "out_gain": out_gain, "emitted_projection": emitted_projection}


def rounded(value):
    return lax.optimization_barrier(value.astype(jnp.bfloat16))

def reference(item_owner, item_row, history_len, event_gap, item_table, norm_gain, in_weight, conv_weight, conv_bias, dt_bias, decay_rate, out_gain, emitted_projection):
    inner_dim = HEADS * HEAD_DIM
    conv_dim = inner_dim + 2 * STATE
    block_count = PAST_ACTIONS // BLOCK
    forward_only = jnp.arange(BLOCK)[:, None] >= jnp.arange(BLOCK)[None, :]

    def one_block(carried, packed):
        streams, in_coef, out_coef, steps, log_decay = packed
        cum_decay = jnp.cumsum(log_decay, axis=0)
        scores = jnp.dot(out_coef, in_coef.T, preferred_element_type=jnp.float32)
        cum_heads = cum_decay.T
        spread = cum_heads[:, :, None] - cum_heads[:, None, :]
        fading = jnp.exp(jnp.where(forward_only, spread, 0.0))
        mixing = rounded(jnp.where(forward_only, scores[None] * fading * steps.T[:, None, :], 0.0))
        local_y = jnp.einsum('hqs,shp->qhp', mixing.astype(jnp.float32), streams.astype(jnp.float32))
        held = rounded(carried).astype(jnp.float32)
        carried_y = jnp.exp(cum_decay)[:, :, None] * jnp.einsum('qn,hpn->qhp', out_coef.astype(jnp.float32), held)
        to_end = jnp.exp(cum_decay[-1:] - cum_decay) * steps
        scaled = rounded(to_end[:, :, None] * streams.astype(jnp.float32)).astype(jnp.float32)
        block_state = jnp.einsum('qhp,qn->hpn', scaled, in_coef.astype(jnp.float32))
        carried = jnp.exp(cum_decay[-1])[:, None, None] * carried + block_state
        return (carried, local_y + carried_y)

    def one_user(packed):
        owners, row_ids, length, gap_values = packed
        item_vec = item_table[owners[:, 0] * ITEMS_DEV + row_ids]
        item_wide = item_vec.astype(jnp.float32)
        normed = rounded(item_wide * lax.rsqrt(lax.optimization_barrier(jnp.mean(item_wide * item_wide, axis=-1, keepdims=True)) + 1e-05) * norm_gain)
        projected = rounded(jnp.dot(normed, in_weight, preferred_element_type=jnp.float32))
        gate_raw = projected[:, :inner_dim].astype(jnp.float32)
        conv_in = projected[:, inner_dim:inner_dim + conv_dim]
        raw_step_size = projected[:, inner_dim + conv_dim:].astype(jnp.float32)
        padded = jnp.pad(conv_in, ((3, 0), (0, 0))).astype(jnp.float32)
        conv_sum = conv_bias + conv_weight[0] * padded[0:PAST_ACTIONS]
        for tap_index in range(1, 4):
            conv_sum = conv_sum + conv_weight[tap_index] * padded[tap_index:tap_index + PAST_ACTIONS]
        conv_out = rounded(jax.nn.silu(conv_sum))
        streams = conv_out[:, :inner_dim].reshape(block_count, BLOCK, HEADS, HEAD_DIM)
        in_coef = conv_out[:, inner_dim:inner_dim + STATE].reshape(block_count, BLOCK, STATE)
        out_coef = conv_out[:, inner_dim + STATE:].reshape(block_count, BLOCK, STATE)
        alive = (jnp.arange(PAST_ACTIONS, dtype=jnp.int32) < length).astype(jnp.float32)
        steps = alive[:, None] * jax.nn.softplus(raw_step_size + dt_bias)
        log_decay = -decay_rate * gap_values[:, None] * steps
        start = jnp.zeros((HEADS, HEAD_DIM, STATE), jnp.float32)
        unused, response = lax.scan(one_block, start, (streams, in_coef, out_coef, steps.reshape(block_count, BLOCK, HEADS), log_decay.reshape(block_count, BLOCK, HEADS)))
        response = response.reshape(PAST_ACTIONS, HEADS, HEAD_DIM)
        gated = response * jax.nn.silu(gate_raw.reshape(PAST_ACTIONS, HEADS, HEAD_DIM))
        gated = gated * lax.rsqrt(lax.optimization_barrier(jnp.mean(gated * gated, axis=-1, keepdims=True)) + 1e-05)
        normed_y = rounded(gated.reshape(PAST_ACTIONS, inner_dim) * out_gain)
        layer_out = item_wide + jnp.dot(normed_y, emitted_projection, preferred_element_type=jnp.float32)
        return (alive[:, None] * layer_out).astype(jnp.bfloat16)
    return lax.map(one_user, (item_owner, item_row, history_len, event_gap))
```

```python
import jax
import jax.numpy as jnp
from jax import lax
from jax.experimental import pallas as pl
from jax.experimental.pallas import tpu as pltpu
from jax.sharding import PartitionSpec as P

BLOCK = 256
F32 = jnp.float32
BF16 = jnp.bfloat16
VMEM_LIMIT = 40 * 1024 * 1024


def passed_along(block, axis, distance):
    devices = range(lax.axis_size(axis))
    route = [(i - distance, i) for i in devices if i - distance in devices]
    return lax.ppermute(block, axis, route)


def head_spread(head_count, inner_dim):
    head_dim = inner_dim // head_count
    lane = lax.broadcasted_iota(jnp.int32, (head_count, inner_dim), 1)
    row = lax.broadcasted_iota(jnp.int32, (head_count, inner_dim), 0)
    first = row * head_dim
    return jnp.where((lane >= first) & (lane < first + head_dim), 1.0, 0.0).astype(BF16)


def over_channels(values, spread):
    high = values.astype(BF16)
    low = (values - high.astype(F32)).astype(BF16)
    return jnp.dot(high, spread, preferred_element_type=F32) + jnp.dot(
        low, spread, preferred_element_type=F32
    )


def silu(v):
    return v / (1.0 + jnp.exp(-v))


def project_kernel(inner_dim, conv_dim, place, rows, gain, weight, item, gate, conv, step):
    count = rows.shape[0]
    lane = lax.broadcasted_iota(jnp.int32, (BLOCK, count), 1)
    hot = jnp.where(lane == place[...], 1.0, 0.0).astype(BF16)
    wide = jnp.dot(hot, rows[...], preferred_element_type=F32)
    item[...] = wide.astype(BF16)
    scale = lax.rsqrt(jnp.mean(wide * wide, axis=-1, keepdims=True) + 1e-05)
    normed = (wide * scale * gain[...]).astype(BF16)
    gate[...] = jnp.dot(normed, weight[:, :inner_dim], preferred_element_type=F32).astype(BF16)
    conv[...] = jnp.dot(
        normed, weight[:, inner_dim : inner_dim + conv_dim], preferred_element_type=F32
    ).astype(BF16)
    step[...] = (
        jnp.dot(normed, weight[:, inner_dim + conv_dim :], preferred_element_type=F32)
        .astype(BF16)
        .astype(F32)
    )


def state_kernel(
    inner_dim, conv, step, gap, alive, edge, taps, bias, dt_bias, rate,
    x_out, bc_out, steps_out, cum_out, entering, before, final, factor,
    padded, running, gone,
):
    head_count = step.shape[1]
    state_dim = entering.shape[1]
    block_index = pl.program_id(0)

    @pl.when(block_index == 0)
    def _():
        padded[0:8] = edge[...].astype(F32)
        running[...] = jnp.zeros_like(running)
        gone[...] = jnp.zeros_like(gone)

    padded[8 : 8 + BLOCK] = conv[...].astype(F32)
    total = bias[...] + taps[0:1] * padded[5 : 5 + BLOCK]
    for k in range(1, 4):
        total = total + taps[k : k + 1] * padded[5 + k : 5 + k + BLOCK]
    padded[0:8] = padded[BLOCK : BLOCK + 8]
    out = silu(total).astype(BF16)
    x = out[:, :inner_dim]
    bc = out[:, inner_dim:]
    x_out[...] = x
    bc_out[...] = bc
    raw = step[...] + dt_bias[...]
    soft = jnp.maximum(raw, 0.0) + jnp.log1p(jnp.exp(-jnp.abs(raw)))
    steps = alive[...] * soft
    log_decay = -rate[...] * gap[...] * steps
    below = lax.broadcasted_iota(jnp.int32, (BLOCK, BLOCK), 0) >= lax.broadcasted_iota(
        jnp.int32, (BLOCK, BLOCK), 1
    )
    cum = jnp.dot(
        jnp.where(below, 1.0, 0.0), log_decay, preferred_element_type=F32,
        precision=lax.Precision.HIGHEST,
    )
    steps_out[...] = steps
    cum_out[...] = cum
    last = cum[BLOCK - 1 : BLOCK]
    spread = head_spread(head_count, inner_dim)
    scaled = (over_channels(jnp.exp(last - cum) * steps, spread) * x.astype(F32)).astype(BF16)
    block_state = lax.dot_general(
        bc[:, :state_dim], scaled, (((0,), (0,)), ((), ())), preferred_element_type=F32
    )
    entering[0] = running[...]
    before[0] = over_channels(jnp.exp(gone[...]), spread)
    fade = over_channels(jnp.broadcast_to(jnp.exp(last), gone.shape), spread)
    new = fade[0:1] * running[...] + block_state
    running[...] = new
    gone[...] = gone[...] + last
    final[...] = new
    factor[...] = over_channels(jnp.exp(gone[...]), spread)


def local_kernel(x, bc, steps, cum, y):
    head_count = steps.shape[1]
    inner_dim = x.shape[1]
    state_dim = bc.shape[1] // 2
    spread = head_spread(head_count, inner_dim)
    xs = (over_channels(steps[...], spread) * x[...].astype(F32)).astype(BF16)
    scores = lax.dot_general(
        bc[:, state_dim:], bc[:, :state_dim], (((1,), (1,)), ((), ())),
        preferred_element_type=F32,
    )
    below = lax.broadcasted_iota(jnp.int32, (BLOCK, BLOCK), 0) >= lax.broadcasted_iota(
        jnp.int32, (BLOCK, BLOCK), 1
    )
    scores = jnp.where(below, scores, 0.0)
    down = cum[...]
    across = down.T
    width = 2 * (inner_dim // head_count)
    left = lax.broadcasted_iota(jnp.int32, (BLOCK, width), 1) < width // 2
    for pair in range(head_count // 2):
        lanes = slice(pair * width, (pair + 1) * width)
        parts = []
        for h in (2 * pair, 2 * pair + 1):
            fading = jnp.exp(jnp.minimum(down[:, h : h + 1] - across[h : h + 1], 0.0))
            mixing = (scores * fading).astype(BF16)
            parts.append(jnp.dot(mixing, xs[:, lanes], preferred_element_type=F32))
        y[:, lanes] = jnp.where(left, parts[0], parts[1])


def emit_kernel(
    y, bc, cum, gate, item, alive, entering, before, incoming, gain, weight, out
):
    head_count = cum.shape[1]
    inner_dim = y.shape[1]
    state_dim = bc.shape[1] // 2
    spread = head_spread(head_count, inner_dim)
    held = (entering[0] + before[0, 0:1] * incoming[...]).astype(BF16)
    carried = jnp.dot(bc[:, state_dim:], held, preferred_element_type=F32)
    response = y[...] + over_channels(jnp.exp(cum[...]), spread) * carried
    gated = response * silu(gate[...].astype(F32))
    squares = lax.dot_general(
        (gated * gated).astype(BF16), spread, (((1,), (1,)), ((), ())),
        preferred_element_type=F32,
    )
    scale = lax.rsqrt(squares * (head_count / inner_dim) + 1e-05)
    normed = (gated * over_channels(scale, spread) * gain[...]).astype(BF16)
    mixed = jnp.dot(normed, weight[...], preferred_element_type=F32)
    out[...] = (alive[...] * (item[...].astype(F32) + mixed)).astype(BF16)


def rows_of(width):
    return pl.BlockSpec((BLOCK, width), lambda i: (i, 0))


def whole(*shape):
    return pl.BlockSpec(shape, lambda i: (0,) * len(shape))


def one_of(*shape):
    return pl.BlockSpec((1, *shape), lambda i: (i,) + (0,) * len(shape))


def params():
    return pltpu.CompilerParams(
        vmem_limit_bytes=VMEM_LIMIT, dimension_semantics=("arbitrary",)
    )


def cost(flops, size, exps=0):
    return pl.CostEstimate(flops=flops, bytes_accessed=size, transcendentals=exps)


def struct(shape, dtype):
    return jax.ShapeDtypeStruct(shape, dtype)


def earlier_spans(state, factor):
    length, here = (lax.axis_size("tm"), lax.axis_index("tm"))
    size = state.shape[0]
    total, fade = (jnp.zeros_like(state), jnp.ones_like(factor))
    distance = 1
    while distance < length:
        own = state + factor * total
        own_fade = factor * fade
        high = own_fade.astype(BF16)
        low = (own_fade - high.astype(F32)).astype(BF16)
        packed = jnp.concatenate([own.astype(BF16), high, low], axis=0)
        got = passed_along(packed, "tm", distance).astype(F32)
        reached = here >= distance
        got_fade = jnp.where(reached, got[size : size + 1] + got[size + 1 : size + 2], 1.0)
        total = total + fade * got[:size]
        fade = fade * got_fade
        distance *= 2
    return total


def per_device(
    item_owner,
    item_row,
    history_len,
    event_gap,
    item_table,
    norm_gain,
    in_weight,
    conv_weight,
    conv_bias,
    dt_bias,
    decay_rate,
    out_gain,
    emitted_projection,
):
    user_count, events = item_row.shape
    model_dim = item_table.shape[1]
    head_count = dt_bias.shape[0]
    inner_dim = emitted_projection.shape[0]
    conv_dim = conv_weight.shape[1]
    state_dim = (conv_dim - inner_dim) // 2
    projected_dim = in_weight.shape[1]
    devices = lax.axis_size("tm") * lax.axis_size("table")
    capacity = max(2 * events // devices, 2)
    blocks = events // BLOCK
    slots_all = devices * capacity

    owners = item_owner[..., 0]
    owner_match = owners[..., None] == jnp.arange(devices, dtype=jnp.int32)
    owner_hot = owner_match.astype(BF16)
    earlier_mask = (jnp.arange(events)[:, None] > jnp.arange(events)[None, :]).astype(BF16)
    earlier_counts = jnp.einsum(
        "ts,usd->utd", earlier_mask, owner_hot, preferred_element_type=F32
    )
    slots = jnp.sum(jnp.where(owner_match, earlier_counts, 0.0), axis=-1).astype(jnp.int32)
    slot_match = slots[..., None] == jnp.arange(capacity, dtype=jnp.int32)
    row_high = item_row // 64
    row_low = item_row - row_high * 64
    parts = jnp.concatenate(
        [
            jnp.where(slot_match, row_high[..., None], 0),
            jnp.where(slot_match, row_low[..., None], 0),
        ],
        axis=-1,
    ).astype(BF16)
    asked = jnp.einsum("utd,utc->duc", owner_hot, parts, preferred_element_type=F32)
    requests = (64.0 * asked[..., :capacity] + asked[..., capacity:]).astype(jnp.int32)
    wanted = lax.all_to_all(requests, ("tm", "table"), split_axis=0, concat_axis=0, tiled=True)
    place = owners * capacity + slots

    positions = lax.axis_index("tm") * events + jnp.arange(events, dtype=jnp.int32)
    alive = (positions[None, :] < history_len[:, None]).astype(F32)

    fetched = []
    for user in range(user_count):
        sent = jnp.take(item_table, wanted[:, user].reshape(-1), axis=0, mode="clip")
        fetched.append(
            lax.all_to_all(
                sent.reshape(devices, capacity, model_dim),
                ("tm", "table"),
                split_axis=0,
                concat_axis=0,
                tiled=True,
            ).reshape(slots_all, model_dim)
        )

    outputs = []
    for user in range(user_count):
        alive_column = alive[user][:, None]
        item, gate, conv, step = pl.pallas_call(
            lambda *refs: project_kernel(inner_dim, conv_dim, *refs),
            grid=(blocks,),
            in_specs=[
                rows_of(1),
                whole(slots_all, model_dim),
                whole(1, model_dim),
                whole(model_dim, projected_dim),
            ],
            out_specs=[rows_of(model_dim), rows_of(inner_dim), rows_of(conv_dim), rows_of(head_count)],
            out_shape=[
                struct((events, model_dim), BF16),
                struct((events, inner_dim), BF16),
                struct((events, conv_dim), BF16),
                struct((events, head_count), F32),
            ],
            compiler_params=params(),
            cost_estimate=cost(2 * events * model_dim * (projected_dim + slots_all), 9 << 20),
            name="project",
        )(place[user][:, None], fetched[user], norm_gain[None], in_weight)
        edge = passed_along(conv[events - 8 :], "tm", 1)
        x, bc, steps, cum, entering, before, final, factor = pl.pallas_call(
            lambda *refs: state_kernel(inner_dim, *refs),
            grid=(blocks,),
            in_specs=[
                rows_of(conv_dim),
                rows_of(head_count),
                rows_of(1),
                rows_of(1),
                whole(8, conv_dim),
                whole(4, conv_dim),
                whole(1, conv_dim),
                whole(1, head_count),
                whole(1, head_count),
            ],
            out_specs=[
                rows_of(inner_dim),
                rows_of(2 * state_dim),
                rows_of(head_count),
                rows_of(head_count),
                one_of(state_dim, inner_dim),
                one_of(8, inner_dim),
                whole(state_dim, inner_dim),
                whole(8, inner_dim),
            ],
            out_shape=[
                struct((events, inner_dim), BF16),
                struct((events, 2 * state_dim), BF16),
                struct((events, head_count), F32),
                struct((events, head_count), F32),
                struct((blocks, state_dim, inner_dim), F32),
                struct((blocks, 8, inner_dim), F32),
                struct((state_dim, inner_dim), F32),
                struct((8, inner_dim), F32),
            ],
            scratch_shapes=[
                pltpu.VMEM((BLOCK + 8, conv_dim), F32),
                pltpu.VMEM((state_dim, inner_dim), F32),
                pltpu.VMEM((8, head_count), F32),
            ],
            compiler_params=params(),
            cost_estimate=cost(4 << 30, 8 << 20, events * conv_dim),
            name="states",
        )(
            conv, step, event_gap[user][:, None], alive_column, edge,
            conv_weight, conv_bias[None], dt_bias[None], decay_rate[None],
        )
        incoming = earlier_spans(final, factor[0:1])
        y = pl.pallas_call(
            local_kernel,
            grid=(blocks,),
            in_specs=[
                rows_of(inner_dim), rows_of(2 * state_dim), rows_of(head_count), rows_of(head_count),
            ],
            out_specs=rows_of(inner_dim),
            out_shape=struct((events, inner_dim), F32),
            compiler_params=params(),
            cost_estimate=cost(8 << 30, 5 << 20, events * BLOCK * head_count),
            name="local",
        )(x, bc, steps, cum)
        outputs.append(
            pl.pallas_call(
                emit_kernel,
                grid=(blocks,),
                in_specs=[
                    rows_of(inner_dim),
                    rows_of(2 * state_dim),
                    rows_of(head_count),
                    rows_of(inner_dim),
                    rows_of(model_dim),
                    rows_of(1),
                    one_of(state_dim, inner_dim),
                    one_of(8, inner_dim),
                    whole(state_dim, inner_dim),
                    whole(1, inner_dim),
                    whole(inner_dim, model_dim),
                ],
                out_specs=rows_of(model_dim),
                out_shape=struct((events, model_dim), BF16),
                compiler_params=params(),
                cost_estimate=cost(4 << 30, 9 << 20, events * inner_dim),
                name="emit",
            )(
                y, bc, cum, gate, item, alive_column, entering, before, incoming,
                out_gain[None], emitted_projection,
            )
        )
    return jnp.stack(outputs)


def solution(mesh):
    in_specs = (
        P("table", "tm", None),
        P("table", "tm"),
        P("table"),
        P("table", "tm"),
        P(("tm", "table"), None),
        P(),
        P(),
        P(),
        P(),
        P(),
        P(),
        P(),
        P(),
    )
    out_specs = P("table", "tm", None)
    return jax.shard_map(
        per_device, mesh=mesh, in_specs=in_specs, out_specs=out_specs, check_vma=False
    )
```

```python
import jax
import jax.numpy as jnp
from jax import lax
from jax.experimental import pallas as pl
from jax.experimental.pallas import tpu as pltpu
from jax.sharding import PartitionSpec as P

BLOCK = 256
F32 = jnp.float32
BF16 = jnp.bfloat16
VMEM_LIMIT = 40 * 1024 * 1024


def passed_along(block, axis, distance):
    devices = range(lax.axis_size(axis))
    route = [(i - distance, i) for i in devices if i - distance in devices]
    return lax.ppermute(block, axis, route)


def head_spread(head_count, inner_dim):
    head_dim = inner_dim // head_count
    lane = lax.broadcasted_iota(jnp.int32, (head_count, inner_dim), 1)
    row = lax.broadcasted_iota(jnp.int32, (head_count, inner_dim), 0)
    first = row * head_dim
    return jnp.where((lane >= first) & (lane < first + head_dim), 1.0, 0.0).astype(BF16)


def over_channels(values, spread):
    high = values.astype(BF16)
    low = (values - high.astype(F32)).astype(BF16)
    return jnp.dot(high, spread, preferred_element_type=F32) + jnp.dot(
        low, spread, preferred_element_type=F32
    )


def silu(v):
    return v / (1.0 + jnp.exp(-v))


def project_kernel(inner_dim, conv_dim, place, rows, gain, weight, item, gate, conv, step):
    count = rows.shape[0]
    lane = lax.broadcasted_iota(jnp.int32, (BLOCK, count), 1)
    hot = jnp.where(lane == place[...], 1.0, 0.0).astype(BF16)
    wide = jnp.dot(hot, rows[...], preferred_element_type=F32)
    item[...] = wide.astype(BF16)
    scale = lax.rsqrt(jnp.mean(wide * wide, axis=-1, keepdims=True) + 1e-05)
    normed = (wide * scale * gain[...]).astype(BF16)
    gate[...] = jnp.dot(normed, weight[:, :inner_dim], preferred_element_type=F32).astype(BF16)
    conv[...] = jnp.dot(
        normed, weight[:, inner_dim : inner_dim + conv_dim], preferred_element_type=F32
    ).astype(BF16)
    step[...] = (
        jnp.dot(normed, weight[:, inner_dim + conv_dim :], preferred_element_type=F32)
        .astype(BF16)
        .astype(F32)
    )


def state_kernel(
    inner_dim, conv, step, gap, alive, edge, taps, bias, dt_bias, rate,
    x_out, bc_out, steps_out, cum_out, entering, before, final, factor,
    padded, running, gone,
):
    head_count = step.shape[1]
    state_dim = entering.shape[1]
    block_index = pl.program_id(0)

    @pl.when(block_index == 0)
    def _():
        padded[0:8] = edge[...].astype(F32)
        running[...] = jnp.zeros_like(running)
        gone[...] = jnp.zeros_like(gone)

    padded[8 : 8 + BLOCK] = conv[...].astype(F32)
    total = bias[...] + taps[0:1] * padded[5 : 5 + BLOCK]
    for k in range(1, 4):
        total = total + taps[k : k + 1] * padded[5 + k : 5 + k + BLOCK]
    padded[0:8] = padded[BLOCK : BLOCK + 8]
    out = silu(total).astype(BF16)
    x = out[:, :inner_dim]
    bc = out[:, inner_dim:]
    x_out[...] = x
    bc_out[...] = bc
    raw = step[...] + dt_bias[...]
    soft = jnp.maximum(raw, 0.0) + jnp.log1p(jnp.exp(-jnp.abs(raw)))
    steps = alive[...] * soft
    log_decay = -rate[...] * gap[...] * steps
    below = lax.broadcasted_iota(jnp.int32, (BLOCK, BLOCK), 0) >= lax.broadcasted_iota(
        jnp.int32, (BLOCK, BLOCK), 1
    )
    cum = jnp.dot(
        jnp.where(below, 1.0, 0.0), log_decay, preferred_element_type=F32,
        precision=lax.Precision.HIGHEST,
    )
    steps_out[...] = steps
    cum_out[...] = cum
    last = cum[BLOCK - 1 : BLOCK]
    spread = head_spread(head_count, inner_dim)
    scaled = (over_channels(jnp.exp(last - cum) * steps, spread) * x.astype(F32)).astype(BF16)
    block_state = lax.dot_general(
        bc[:, :state_dim], scaled, (((0,), (0,)), ((), ())), preferred_element_type=F32
    )
    entering[0] = running[...]
    before[0] = over_channels(jnp.exp(gone[...]), spread)
    fade = over_channels(jnp.broadcast_to(jnp.exp(last), gone.shape), spread)
    new = fade[0:1] * running[...] + block_state
    running[...] = new
    gone[...] = gone[...] + last
    final[...] = new
    factor[...] = over_channels(jnp.exp(gone[...]), spread)


def local_kernel(x, bc, steps, cum, y):
    head_count = steps.shape[1]
    inner_dim = x.shape[1]
    state_dim = bc.shape[1] // 2
    spread = head_spread(head_count, inner_dim)
    xs = (over_channels(steps[...], spread) * x[...].astype(F32)).astype(BF16)
    scores = lax.dot_general(
        bc[:, state_dim:], bc[:, :state_dim], (((1,), (1,)), ((), ())),
        preferred_element_type=F32,
    )
    below = lax.broadcasted_iota(jnp.int32, (BLOCK, BLOCK), 0) >= lax.broadcasted_iota(
        jnp.int32, (BLOCK, BLOCK), 1
    )
    scores = jnp.where(below, scores, 0.0)
    down = cum[...]
    across = down.T
    width = 2 * (inner_dim // head_count)
    left = lax.broadcasted_iota(jnp.int32, (BLOCK, width), 1) < width // 2
    for pair in range(head_count // 2):
        lanes = slice(pair * width, (pair + 1) * width)
        parts = []
        for h in (2 * pair, 2 * pair + 1):
            fading = jnp.exp(jnp.minimum(down[:, h : h + 1] - across[h : h + 1], 0.0))
            mixing = (scores * fading).astype(BF16)
            parts.append(jnp.dot(mixing, xs[:, lanes], preferred_element_type=F32))
        y[:, lanes] = jnp.where(left, parts[0], parts[1])


def emit_kernel(
    y, bc, cum, gate, item, alive, entering, before, incoming, gain, weight, *rest
):
    out = rest[-1]
    head_count = cum.shape[1]
    inner_dim = y.shape[1]
    state_dim = bc.shape[1] // 2
    spread = head_spread(head_count, inner_dim)
    held = (entering[0] + before[0, 0:1] * incoming[...]).astype(BF16)
    carried = jnp.dot(bc[:, state_dim:], held, preferred_element_type=F32)
    response = y[...] + over_channels(jnp.exp(cum[...]), spread) * carried
    gated = response * silu(gate[...].astype(F32))
    squares = lax.dot_general(
        (gated * gated).astype(BF16), spread, (((1,), (1,)), ((), ())),
        preferred_element_type=F32,
    )
    scale = lax.rsqrt(squares * (head_count / inner_dim) + 1e-05)
    normed = (gated * over_channels(scale, spread) * gain[...]).astype(BF16)
    mixed = jnp.dot(normed, weight[...], preferred_element_type=F32)
    out[...] = (alive[...] * (item[...].astype(F32) + mixed)).astype(BF16)


def rows_of(width):
    return pl.BlockSpec((BLOCK, width), lambda i: (i, 0))


def whole(*shape):
    return pl.BlockSpec(shape, lambda i: (0,) * len(shape))


def one_of(*shape):
    return pl.BlockSpec((1, *shape), lambda i: (i,) + (0,) * len(shape))


def params():
    return pltpu.CompilerParams(
        vmem_limit_bytes=VMEM_LIMIT, dimension_semantics=("arbitrary",)
    )


def cost(flops, size, exps=0):
    return pl.CostEstimate(flops=flops, bytes_accessed=size, transcendentals=exps)


def struct(shape, dtype):
    return jax.ShapeDtypeStruct(shape, dtype)


def earlier_spans(state, factor):
    length, here = (lax.axis_size("tm"), lax.axis_index("tm"))
    size = state.shape[0]
    total, fade = (jnp.zeros_like(state), jnp.ones_like(factor))
    distance = 1
    while distance < length:
        own = state + factor * total
        own_fade = factor * fade
        high = own_fade.astype(BF16)
        low = (own_fade - high.astype(F32)).astype(BF16)
        packed = jnp.concatenate([own.astype(BF16), high, low], axis=0)
        got = passed_along(packed, "tm", distance).astype(F32)
        reached = here >= distance
        got_fade = jnp.where(reached, got[size : size + 1] + got[size + 1 : size + 2], 1.0)
        total = total + fade * got[:size]
        fade = fade * got_fade
        distance *= 2
    return total


def per_device(
    item_owner,
    item_row,
    history_len,
    event_gap,
    item_table,
    norm_gain,
    in_weight,
    conv_weight,
    conv_bias,
    dt_bias,
    decay_rate,
    out_gain,
    emitted_projection,
):
    user_count, events = item_row.shape
    model_dim = item_table.shape[1]
    head_count = dt_bias.shape[0]
    inner_dim = emitted_projection.shape[0]
    conv_dim = conv_weight.shape[1]
    state_dim = (conv_dim - inner_dim) // 2
    projected_dim = in_weight.shape[1]
    devices = lax.axis_size("tm") * lax.axis_size("table")
    capacity = max(2 * events // devices, 2)
    blocks = events // BLOCK
    slots_all = devices * capacity

    owners = item_owner[..., 0]
    owner_match = owners[..., None] == jnp.arange(devices, dtype=jnp.int32)
    owner_hot = owner_match.astype(BF16)
    earlier_mask = (jnp.arange(events)[:, None] > jnp.arange(events)[None, :]).astype(BF16)
    earlier_counts = jnp.einsum(
        "ts,usd->utd", earlier_mask, owner_hot, preferred_element_type=F32
    )
    slots = jnp.sum(jnp.where(owner_match, earlier_counts, 0.0), axis=-1).astype(jnp.int32)
    slot_match = slots[..., None] == jnp.arange(capacity, dtype=jnp.int32)
    row_high = item_row // 64
    row_low = item_row - row_high * 64
    parts = jnp.concatenate(
        [
            jnp.where(slot_match, row_high[..., None], 0),
            jnp.where(slot_match, row_low[..., None], 0),
        ],
        axis=-1,
    ).astype(BF16)
    asked = jnp.einsum("utd,utc->duc", owner_hot, parts, preferred_element_type=F32)
    requests = (64.0 * asked[..., :capacity] + asked[..., capacity:]).astype(jnp.int32)
    wanted = lax.all_to_all(requests, ("tm", "table"), split_axis=0, concat_axis=0, tiled=True)
    place = owners * capacity + slots

    positions = lax.axis_index("tm") * events + jnp.arange(events, dtype=jnp.int32)
    alive = (positions[None, :] < history_len[:, None]).astype(F32)

    fetched = []
    for user in range(user_count):
        sent = jnp.take(item_table, wanted[:, user].reshape(-1), axis=0, mode="clip")
        fetched.append(
            lax.all_to_all(
                sent.reshape(devices, capacity, model_dim),
                ("tm", "table"),
                split_axis=0,
                concat_axis=0,
                tiled=True,
            ).reshape(slots_all, model_dim)
        )

    result = None
    for user in range(user_count):
        if result is not None:
            fetched[user], result = lax.optimization_barrier((fetched[user], result))
        alive_column = alive[user][:, None]
        item, gate, conv, step = pl.pallas_call(
            lambda *refs: project_kernel(inner_dim, conv_dim, *refs),
            grid=(blocks,),
            in_specs=[
                rows_of(1),
                whole(slots_all, model_dim),
                whole(1, model_dim),
                whole(model_dim, projected_dim),
            ],
            out_specs=[rows_of(model_dim), rows_of(inner_dim), rows_of(conv_dim), rows_of(head_count)],
            out_shape=[
                struct((events, model_dim), BF16),
                struct((events, inner_dim), BF16),
                struct((events, conv_dim), BF16),
                struct((events, head_count), F32),
            ],
            compiler_params=params(),
            cost_estimate=cost(2 * events * model_dim * (projected_dim + slots_all), 9 << 20),
            name="project",
        )(place[user][:, None], fetched[user], norm_gain[None], in_weight)
        edge = passed_along(conv[events - 8 :], "tm", 1)
        x, bc, steps, cum, entering, before, final, factor = pl.pallas_call(
            lambda *refs: state_kernel(inner_dim, *refs),
            grid=(blocks,),
            in_specs=[
                rows_of(conv_dim),
                rows_of(head_count),
                rows_of(1),
                rows_of(1),
                whole(8, conv_dim),
                whole(4, conv_dim),
                whole(1, conv_dim),
                whole(1, head_count),
                whole(1, head_count),
            ],
            out_specs=[
                rows_of(inner_dim),
                rows_of(2 * state_dim),
                rows_of(head_count),
                rows_of(head_count),
                one_of(state_dim, inner_dim),
                one_of(8, inner_dim),
                whole(state_dim, inner_dim),
                whole(8, inner_dim),
            ],
            out_shape=[
                struct((events, inner_dim), BF16),
                struct((events, 2 * state_dim), BF16),
                struct((events, head_count), F32),
                struct((events, head_count), F32),
                struct((blocks, state_dim, inner_dim), F32),
                struct((blocks, 8, inner_dim), F32),
                struct((state_dim, inner_dim), F32),
                struct((8, inner_dim), F32),
            ],
            scratch_shapes=[
                pltpu.VMEM((BLOCK + 8, conv_dim), F32),
                pltpu.VMEM((state_dim, inner_dim), F32),
                pltpu.VMEM((8, head_count), F32),
            ],
            compiler_params=params(),
            cost_estimate=cost(4 << 30, 8 << 20, events * conv_dim),
            name="states",
        )(
            conv, step, event_gap[user][:, None], alive_column, edge,
            conv_weight, conv_bias[None], dt_bias[None], decay_rate[None],
        )
        incoming = earlier_spans(final, factor[0:1])
        y = pl.pallas_call(
            local_kernel,
            grid=(blocks,),
            in_specs=[
                rows_of(inner_dim), rows_of(2 * state_dim), rows_of(head_count), rows_of(head_count),
            ],
            out_specs=rows_of(inner_dim),
            out_shape=struct((events, inner_dim), F32),
            compiler_params=params(),
            cost_estimate=cost(8 << 30, 5 << 20, events * BLOCK * head_count),
            name="local",
        )(x, bc, steps, cum)
        in_specs = [
            rows_of(inner_dim),
            rows_of(2 * state_dim),
            rows_of(head_count),
            rows_of(inner_dim),
            rows_of(model_dim),
            rows_of(1),
            one_of(state_dim, inner_dim),
            one_of(8, inner_dim),
            whole(state_dim, inner_dim),
            whole(1, inner_dim),
            whole(inner_dim, model_dim),
        ]
        operands = [
            y, bc, cum, gate, item, alive_column, entering, before, incoming,
            out_gain[None], emitted_projection,
        ]
        aliases = {}
        if result is not None:
            aliases = {len(operands): 0}
            operands.append(result)
            in_specs.append(pl.BlockSpec(memory_space=pl.ANY))
        result = pl.pallas_call(
            emit_kernel,
            grid=(blocks,),
            in_specs=in_specs,
            out_specs=pl.BlockSpec((None, BLOCK, model_dim), lambda i, user=user: (user, i, 0)),
            out_shape=struct((user_count, events, model_dim), BF16),
            input_output_aliases=aliases,
            compiler_params=params(),
            cost_estimate=cost(4 << 30, 9 << 20, events * inner_dim),
            name="emit",
        )(*operands)
    return result


def solution(mesh):
    in_specs = (
        P("table", "tm", None),
        P("table", "tm"),
        P("table"),
        P("table", "tm"),
        P(("tm", "table"), None),
        P(),
        P(),
        P(),
        P(),
        P(),
        P(),
        P(),
        P(),
    )
    out_specs = P("table", "tm", None)
    return jax.shard_map(
        per_device, mesh=mesh, in_specs=in_specs, out_specs=out_specs, check_vma=False
    )
```

```python
import jax
import jax.numpy as jnp
from jax import lax
from jax.experimental import pallas as pl
from jax.experimental.pallas import tpu as pltpu
from jax.sharding import PartitionSpec as P

BLOCK = 256
F32 = jnp.float32
BF16 = jnp.bfloat16
VMEM_LIMIT = 40 * 1024 * 1024


def passed_along(block, axis, distance):
    devices = range(lax.axis_size(axis))
    route = [(i - distance, i) for i in devices if i - distance in devices]
    return lax.ppermute(block, axis, route)


def head_spread(head_count, inner_dim):
    head_dim = inner_dim // head_count
    lane = lax.broadcasted_iota(jnp.int32, (head_count, inner_dim), 1)
    row = lax.broadcasted_iota(jnp.int32, (head_count, inner_dim), 0)
    first = row * head_dim
    return jnp.where((lane >= first) & (lane < first + head_dim), 1.0, 0.0).astype(BF16)


def over_channels(values, spread):
    high = values.astype(BF16)
    low = (values - high.astype(F32)).astype(BF16)
    return jnp.dot(high, spread, preferred_element_type=F32) + jnp.dot(
        low, spread, preferred_element_type=F32
    )


def silu(v):
    return v / (1.0 + jnp.exp(-v))


def exchange_kernel(
    count, group, requests, table_hbm, fetched,
    table, asked, wanted, ready, table_sem, self_sem, ask_send, ask_recv, row_send, row_recv,
):
    tm, across = (lax.axis_index("tm"), lax.axis_index("table"))
    width = lax.axis_size("table")
    me = tm * width + across
    half = count // 2

    def device(index):
        return (index // width, index % width)

    def ask(k):
        target = (me + k) % count
        return pltpu.make_async_remote_copy(
            src_ref=requests.at[target],
            dst_ref=wanted.at[k],
            send_sem=ask_send.at[k],
            recv_sem=ask_recv.at[k],
            device_id=device(target),
            device_id_type=pl.DeviceIdType.MESH,
        )

    def give(k):
        return pltpu.make_async_remote_copy(
            src_ref=ready.at[:, k],
            dst_ref=fetched.at[:, k],
            send_sem=row_send.at[k],
            recv_sem=row_recv.at[k],
            device_id=device((me + count - k) % count),
            device_id_type=pl.DeviceIdType.MESH,
        )

    asked[...] = jnp.zeros_like(asked)
    loading = pltpu.make_async_copy(table_hbm, table, table_sem)
    loading.start()
    own_ask = pltpu.make_async_copy(requests.at[me], wanted.at[0], self_sem)
    own_ask.start()
    barrier = pltpu.get_barrier_semaphore()

    @pl.loop(1, count)
    def _(k):
        pl.semaphore_signal(
            barrier, inc=1, device_id=device((me + k) % count),
            device_id_type=pl.DeviceIdType.MESH,
        )

    pl.semaphore_wait(barrier, count - 1)

    def kth(p):
        return jnp.where(p % 2 == 0, half + p // 2, ((p + 1) // 2) % half)

    @pl.loop(0, count - 1)
    def _(p):
        ask(kth(p)).start()

    own_ask.wait()
    loading.wait()
    users, _, slots, _ = ready.shape
    lanes = users * slots
    rows = table.shape[0]

    @pl.loop(0, count // group)
    def _(g):
        for j in range(group):
            k = kth(g * group + j)

            @pl.when(k != 0)
            def _():
                ask(k).wait_recv()

            asked[j : j + 1] = wanted[k].astype(F32)
        columns = asked[...].T
        hot = []
        lane = lax.broadcasted_iota(jnp.int32, (lanes, rows), 1)
        for j in range(group):
            column = columns[:lanes, j : j + 1].astype(jnp.int32)
            hot.append(jnp.where(lane == column, 1.0, 0.0).astype(BF16))
        found = jnp.dot(jnp.concatenate(hot, axis=0), table[...], preferred_element_type=F32)
        found = found.astype(BF16)
        for j in range(group):
            k = kth(g * group + j)
            for user in range(users):
                start = j * lanes + user * slots
                ready[user, k] = found[start : start + slots]

            @pl.when(k != 0)
            def _():
                give(k).start()

    own = pltpu.make_async_copy(ready.at[:, 0], fetched.at[:, 0], self_sem)
    own.start()

    @pl.loop(1, count)
    def _(k):
        ask(k).wait_send()
        give(k).wait()

    own.wait()


def project_kernel(inner_dim, conv_dim, place, rows, gain, weight, item, gate, conv, step):
    count = rows.shape[0]
    lane = lax.broadcasted_iota(jnp.int32, (BLOCK, count), 1)
    hot = jnp.where(lane == place[...], 1.0, 0.0).astype(BF16)
    wide = jnp.dot(hot, rows[...], preferred_element_type=F32)
    item[...] = wide.astype(BF16)
    scale = lax.rsqrt(jnp.mean(wide * wide, axis=-1, keepdims=True) + 1e-05)
    normed = (wide * scale * gain[...]).astype(BF16)
    gate[...] = jnp.dot(normed, weight[:, :inner_dim], preferred_element_type=F32).astype(BF16)
    conv[...] = jnp.dot(
        normed, weight[:, inner_dim : inner_dim + conv_dim], preferred_element_type=F32
    ).astype(BF16)
    step[...] = (
        jnp.dot(normed, weight[:, inner_dim + conv_dim :], preferred_element_type=F32)
        .astype(BF16)
        .astype(F32)
    )


def state_kernel(
    inner_dim, conv, step, gap, alive, edge, taps, bias, dt_bias, rate,
    x_out, bc_out, steps_out, cum_out, entering, before, final, factor,
    padded, running, gone,
):
    head_count = step.shape[1]
    state_dim = entering.shape[1]
    block_index = pl.program_id(1)

    @pl.when(block_index == 0)
    def _():
        padded[0:8] = edge[...].astype(F32)
        running[...] = jnp.zeros_like(running)
        gone[...] = jnp.zeros_like(gone)

    padded[8 : 8 + BLOCK] = conv[...].astype(F32)
    total = bias[...] + taps[0:1] * padded[5 : 5 + BLOCK]
    for k in range(1, 4):
        total = total + taps[k : k + 1] * padded[5 + k : 5 + k + BLOCK]
    padded[0:8] = padded[BLOCK : BLOCK + 8]
    out = silu(total).astype(BF16)
    x = out[:, :inner_dim]
    bc = out[:, inner_dim:]
    x_out[...] = x
    bc_out[...] = bc
    raw = step[...] + dt_bias[...]
    soft = jnp.maximum(raw, 0.0) + jnp.log1p(jnp.exp(-jnp.abs(raw)))
    steps = alive[...] * soft
    log_decay = -rate[...] * gap[...] * steps
    below = lax.broadcasted_iota(jnp.int32, (BLOCK, BLOCK), 0) >= lax.broadcasted_iota(
        jnp.int32, (BLOCK, BLOCK), 1
    )
    cum = jnp.dot(
        jnp.where(below, 1.0, 0.0), log_decay, preferred_element_type=F32,
        precision=lax.Precision.HIGHEST,
    )
    steps_out[...] = steps
    cum_out[...] = cum
    last = cum[BLOCK - 1 : BLOCK]
    spread = head_spread(head_count, inner_dim)
    scaled = (over_channels(jnp.exp(last - cum) * steps, spread) * x.astype(F32)).astype(BF16)
    block_state = lax.dot_general(
        bc[:, :state_dim], scaled, (((0,), (0,)), ((), ())), preferred_element_type=F32
    )
    entering[0] = running[...]
    before[0] = over_channels(jnp.exp(gone[...]), spread)
    fade = over_channels(jnp.broadcast_to(jnp.exp(last), gone.shape), spread)
    new = fade[0:1] * running[...] + block_state
    running[...] = new
    gone[...] = gone[...] + last
    final[...] = new
    factor[...] = over_channels(jnp.exp(gone[...]), spread)


def local_kernel(x, bc, steps, cum, y):
    head_count = steps.shape[1]
    inner_dim = x.shape[1]
    state_dim = bc.shape[1] // 2
    spread = head_spread(head_count, inner_dim)
    xs = (over_channels(steps[...], spread) * x[...].astype(F32)).astype(BF16)
    scores = lax.dot_general(
        bc[:, state_dim:], bc[:, :state_dim], (((1,), (1,)), ((), ())),
        preferred_element_type=F32,
    )
    below = lax.broadcasted_iota(jnp.int32, (BLOCK, BLOCK), 0) >= lax.broadcasted_iota(
        jnp.int32, (BLOCK, BLOCK), 1
    )
    scores = jnp.where(below, scores, 0.0)
    down = cum[...]
    across = down.T
    width = 2 * (inner_dim // head_count)
    left = lax.broadcasted_iota(jnp.int32, (BLOCK, width), 1) < width // 2
    for pair in range(head_count // 2):
        lanes = slice(pair * width, (pair + 1) * width)
        parts = []
        for h in (2 * pair, 2 * pair + 1):
            fading = jnp.exp(jnp.minimum(down[:, h : h + 1] - across[h : h + 1], 0.0))
            mixing = (scores * fading).astype(BF16)
            parts.append(jnp.dot(mixing, xs[:, lanes], preferred_element_type=F32))
        y[:, lanes] = jnp.where(left, parts[0], parts[1])


def emit_kernel(
    y, bc, cum, gate, item, alive, entering, before, incoming, gain, weight, out
):
    head_count = cum.shape[1]
    inner_dim = y.shape[1]
    state_dim = bc.shape[1] // 2
    spread = head_spread(head_count, inner_dim)
    held = (entering[0] + before[0, 0:1] * incoming[...]).astype(BF16)
    carried = jnp.dot(bc[:, state_dim:], held, preferred_element_type=F32)
    response = y[...] + over_channels(jnp.exp(cum[...]), spread) * carried
    gated = response * silu(gate[...].astype(F32))
    squares = lax.dot_general(
        (gated * gated).astype(BF16), spread, (((1,), (1,)), ((), ())),
        preferred_element_type=F32,
    )
    scale = lax.rsqrt(squares * (head_count / inner_dim) + 1e-05)
    normed = (gated * over_channels(scale, spread) * gain[...]).astype(BF16)
    mixed = jnp.dot(normed, weight[...], preferred_element_type=F32)
    out[...] = (alive[...] * (item[...].astype(F32) + mixed)).astype(BF16)


def rows_of(width):
    return pl.BlockSpec((None, BLOCK, width), lambda u, i: (u, i, 0))


def whole(*shape):
    return pl.BlockSpec(shape, lambda u, i: (0,) * len(shape))


def user_of(*shape):
    return pl.BlockSpec((None, *shape), lambda u, i: (u,) + (0,) * len(shape))


def one_of(*shape):
    return pl.BlockSpec((None, 1, *shape), lambda u, i: (u, i) + (0,) * len(shape))


def params():
    return pltpu.CompilerParams(
        vmem_limit_bytes=VMEM_LIMIT, dimension_semantics=("arbitrary", "arbitrary")
    )


def cost(flops, size, exps=0):
    return pl.CostEstimate(flops=flops, bytes_accessed=size, transcendentals=exps)


def struct(shape, dtype):
    return jax.ShapeDtypeStruct(shape, dtype)


def earlier_spans(state, factor):
    length, here = (lax.axis_size("tm"), lax.axis_index("tm"))
    size = state.shape[1]
    total, fade = (jnp.zeros_like(state), jnp.ones_like(factor))
    distance = 1
    while distance < length:
        own = state + factor * total
        own_fade = factor * fade
        high = own_fade.astype(BF16)
        low = (own_fade - high.astype(F32)).astype(BF16)
        packed = jnp.concatenate([own.astype(BF16), high, low], axis=1)
        got = passed_along(packed, "tm", distance).astype(F32)
        reached = here >= distance
        got_fade = jnp.where(reached, got[:, size : size + 1] + got[:, size + 1 : size + 2], 1.0)
        total = total + fade * got[:, :size]
        fade = fade * got_fade
        distance *= 2
    return total


def per_device(
    item_owner,
    item_row,
    history_len,
    event_gap,
    item_table,
    norm_gain,
    in_weight,
    conv_weight,
    conv_bias,
    dt_bias,
    decay_rate,
    out_gain,
    emitted_projection,
):
    user_count, events = item_row.shape
    model_dim = item_table.shape[1]
    head_count = dt_bias.shape[0]
    inner_dim = emitted_projection.shape[0]
    conv_dim = conv_weight.shape[1]
    state_dim = (conv_dim - inner_dim) // 2
    projected_dim = in_weight.shape[1]
    devices = lax.axis_size("tm") * lax.axis_size("table")
    capacity = max(2 * events // devices, 2)
    blocks = events // BLOCK

    owners = item_owner[..., 0]
    owner_match = owners[..., None] == jnp.arange(devices, dtype=jnp.int32)
    owner_hot = owner_match.astype(BF16)
    earlier_mask = (jnp.arange(events)[:, None] > jnp.arange(events)[None, :]).astype(BF16)
    earlier_counts = jnp.einsum(
        "ts,usd->utd", earlier_mask, owner_hot, preferred_element_type=F32
    )
    slots = jnp.sum(jnp.where(owner_match, earlier_counts, 0.0), axis=-1).astype(jnp.int32)
    slot_match = slots[..., None] == jnp.arange(capacity, dtype=jnp.int32)
    row_high = item_row // 64
    row_low = item_row - row_high * 64
    parts = jnp.concatenate(
        [
            jnp.where(slot_match, row_high[..., None], 0),
            jnp.where(slot_match, row_low[..., None], 0),
        ],
        axis=-1,
    ).astype(BF16)
    asked = jnp.einsum("utd,utc->duc", owner_hot, parts, preferred_element_type=F32)
    requests = (64.0 * asked[..., :capacity] + asked[..., capacity:]).astype(jnp.int32)
    slot_rows = -(-capacity // 16) * 16
    slots_all = devices * slot_rows
    requests = jnp.pad(requests, ((0, 0), (0, 0), (0, slot_rows - capacity)))
    requests = requests.reshape(devices, 1, user_count * slot_rows)
    lanes = -(-user_count * slot_rows // 128) * 128
    requests = jnp.pad(requests, ((0, 0), (0, 0), (0, lanes - user_count * slot_rows)))
    here = lax.axis_index("tm") * lax.axis_size("table") + lax.axis_index("table")
    place = ((owners - here) % devices) * slot_rows + slots
    group = 4
    buffer = (user_count, devices, slot_rows, model_dim)
    fetched = pl.pallas_call(
        lambda *refs: exchange_kernel(devices, group, *refs),
        in_specs=[pl.BlockSpec(memory_space=pltpu.VMEM), pl.BlockSpec(memory_space=pl.ANY)],
        out_specs=pl.BlockSpec(memory_space=pl.ANY),
        out_shape=struct(buffer, BF16),
        scratch_shapes=[
            pltpu.VMEM(item_table.shape, BF16),
            pltpu.VMEM((8, lanes), F32),
            pltpu.VMEM((devices, 1, lanes), jnp.int32),
            pltpu.VMEM(buffer, BF16),
            pltpu.SemaphoreType.DMA,
            pltpu.SemaphoreType.DMA,
            pltpu.SemaphoreType.DMA((devices,)),
            pltpu.SemaphoreType.DMA((devices,)),
            pltpu.SemaphoreType.DMA((devices,)),
            pltpu.SemaphoreType.DMA((devices,)),
        ],
        compiler_params=pltpu.CompilerParams(
            vmem_limit_bytes=VMEM_LIMIT, collective_id=0, has_side_effects=True
        ),
        cost_estimate=cost(13 << 30, 10 << 20),
        name="exchange",
    )(requests, item_table).reshape(user_count, slots_all, model_dim)

    positions = lax.axis_index("tm") * events + jnp.arange(events, dtype=jnp.int32)
    alive = (positions[None, :] < history_len[:, None]).astype(F32)

    alive_column = alive[..., None]
    item, gate, conv, step = pl.pallas_call(
        lambda *refs: project_kernel(inner_dim, conv_dim, *refs),
        grid=(user_count, blocks),
        in_specs=[
            rows_of(1),
            user_of(slots_all, model_dim),
            whole(1, model_dim),
            whole(model_dim, projected_dim),
        ],
        out_specs=[rows_of(model_dim), rows_of(inner_dim), rows_of(conv_dim), rows_of(head_count)],
        out_shape=[
            struct((user_count, events, model_dim), BF16),
            struct((user_count, events, inner_dim), BF16),
            struct((user_count, events, conv_dim), BF16),
            struct((user_count, events, head_count), F32),
        ],
        compiler_params=params(),
        cost_estimate=cost(2 * events * model_dim * (projected_dim + slots_all), 9 << 20),
        name="project",
    )(place[..., None], fetched, norm_gain[None], in_weight)
    edge = passed_along(conv[:, events - 8 :], "tm", 1)
    x, bc, steps, cum, entering, before, final, factor = pl.pallas_call(
        lambda *refs: state_kernel(inner_dim, *refs),
        grid=(user_count, blocks),
        in_specs=[
            rows_of(conv_dim),
            rows_of(head_count),
            rows_of(1),
            rows_of(1),
            user_of(8, conv_dim),
            whole(4, conv_dim),
            whole(1, conv_dim),
            whole(1, head_count),
            whole(1, head_count),
        ],
        out_specs=[
            rows_of(inner_dim),
            rows_of(2 * state_dim),
            rows_of(head_count),
            rows_of(head_count),
            one_of(state_dim, inner_dim),
            one_of(8, inner_dim),
            user_of(state_dim, inner_dim),
            user_of(8, inner_dim),
        ],
        out_shape=[
            struct((user_count, events, inner_dim), BF16),
            struct((user_count, events, 2 * state_dim), BF16),
            struct((user_count, events, head_count), F32),
            struct((user_count, events, head_count), F32),
            struct((user_count, blocks, state_dim, inner_dim), F32),
            struct((user_count, blocks, 8, inner_dim), F32),
            struct((user_count, state_dim, inner_dim), F32),
            struct((user_count, 8, inner_dim), F32),
        ],
        scratch_shapes=[
            pltpu.VMEM((BLOCK + 8, conv_dim), F32),
            pltpu.VMEM((state_dim, inner_dim), F32),
            pltpu.VMEM((8, head_count), F32),
        ],
        compiler_params=params(),
        cost_estimate=cost(4 << 30, 8 << 20, events * conv_dim),
        name="states",
    )(
        conv, step, event_gap[..., None], alive_column, edge,
        conv_weight, conv_bias[None], dt_bias[None], decay_rate[None],
    )
    incoming = earlier_spans(final, factor[:, 0:1])
    y = pl.pallas_call(
        local_kernel,
        grid=(user_count, blocks),
        in_specs=[
            rows_of(inner_dim), rows_of(2 * state_dim), rows_of(head_count), rows_of(head_count),
        ],
        out_specs=rows_of(inner_dim),
        out_shape=struct((user_count, events, inner_dim), F32),
        compiler_params=params(),
        cost_estimate=cost(8 << 30, 5 << 20, events * BLOCK * head_count),
        name="local",
    )(x, bc, steps, cum)
    return (
        pl.pallas_call(
            emit_kernel,
            grid=(user_count, blocks),
            in_specs=[
                rows_of(inner_dim),
                rows_of(2 * state_dim),
                rows_of(head_count),
                rows_of(inner_dim),
                rows_of(model_dim),
                rows_of(1),
                one_of(state_dim, inner_dim),
                one_of(8, inner_dim),
                user_of(state_dim, inner_dim),
                whole(1, inner_dim),
                whole(inner_dim, model_dim),
            ],
            out_specs=rows_of(model_dim),
            out_shape=struct((user_count, events, model_dim), BF16),
            compiler_params=params(),
            cost_estimate=cost(4 << 30, 9 << 20, events * inner_dim),
            name="emit",
        )(
            y, bc, cum, gate, item, alive_column, entering, before, incoming,
            out_gain[None], emitted_projection,
        )
    )


def solution(mesh):
    in_specs = (
        P("table", "tm", None),
        P("table", "tm"),
        P("table"),
        P("table", "tm"),
        P(("tm", "table"), None),
        P(),
        P(),
        P(),
        P(),
        P(),
        P(),
        P(),
        P(),
    )
    out_specs = P("table", "tm", None)
    return jax.shard_map(
        per_device, mesh=mesh, in_specs=in_specs, out_specs=out_specs, check_vma=False
    )
```

```python
import jax
import jax.numpy as jnp
from jax import lax
from jax.experimental import pallas as pl
from jax.experimental.pallas import tpu as pltpu
from jax.sharding import PartitionSpec as P

BLOCK = 256
F32 = jnp.float32
BF16 = jnp.bfloat16
VMEM_LIMIT = 40 * 1024 * 1024


def passed_along(block, axis, distance):
    devices = range(lax.axis_size(axis))
    route = [(i - distance, i) for i in devices if i - distance in devices]
    return lax.ppermute(block, axis, route)


def head_spread(head_count, inner_dim):
    head_dim = inner_dim // head_count
    lane = lax.broadcasted_iota(jnp.int32, (head_count, inner_dim), 1)
    row = lax.broadcasted_iota(jnp.int32, (head_count, inner_dim), 0)
    first = row * head_dim
    return jnp.where((lane >= first) & (lane < first + head_dim), 1.0, 0.0).astype(BF16)


def over_channels(values, spread):
    high = values.astype(BF16)
    low = (values - high.astype(F32)).astype(BF16)
    return jnp.dot(high, spread, preferred_element_type=F32) + jnp.dot(
        low, spread, preferred_element_type=F32
    )


def silu(v):
    return v / (1.0 + jnp.exp(-v))


def exchange_kernel(
    count, group, requests, table_hbm, fetched,
    table, asked, wanted, ready, table_sem, self_sem, ask_send, ask_recv, row_send, row_recv,
):
    tm, across = (lax.axis_index("tm"), lax.axis_index("table"))
    width = lax.axis_size("table")
    me = tm * width + across
    half = count // 2

    def device(index):
        return (index // width, index % width)

    def ask(k):
        target = (me + k) % count
        return pltpu.make_async_remote_copy(
            src_ref=requests.at[target],
            dst_ref=wanted.at[k],
            send_sem=ask_send.at[k],
            recv_sem=ask_recv.at[k],
            device_id=device(target),
            device_id_type=pl.DeviceIdType.MESH,
        )

    def give(k):
        return pltpu.make_async_remote_copy(
            src_ref=ready.at[:, k],
            dst_ref=fetched.at[:, k],
            send_sem=row_send.at[k],
            recv_sem=row_recv.at[k],
            device_id=device((me + count - k) % count),
            device_id_type=pl.DeviceIdType.MESH,
        )

    asked[...] = jnp.zeros_like(asked)
    loading = pltpu.make_async_copy(table_hbm, table, table_sem)
    loading.start()
    own_ask = pltpu.make_async_copy(requests.at[me], wanted.at[0], self_sem)
    own_ask.start()
    barrier = pltpu.get_barrier_semaphore()

    @pl.loop(1, count)
    def _(k):
        pl.semaphore_signal(
            barrier, inc=1, device_id=device((me + k) % count),
            device_id_type=pl.DeviceIdType.MESH,
        )

    pl.semaphore_wait(barrier, count - 1)

    def kth(p):
        return jnp.where(p % 2 == 0, half + p // 2, ((p + 1) // 2) % half)

    @pl.loop(0, count - 1)
    def _(p):
        ask(kth(p)).start()

    own_ask.wait()
    loading.wait()
    users, _, slots, _ = ready.shape
    lanes = users * slots
    rows = table.shape[0]

    @pl.loop(0, count // group)
    def _(g):
        for j in range(group):
            k = kth(g * group + j)

            @pl.when(k != 0)
            def _():
                ask(k).wait_recv()

            asked[j : j + 1] = wanted[k].astype(F32)
        columns = asked[...].T
        hot = []
        lane = lax.broadcasted_iota(jnp.int32, (lanes, rows), 1)
        for j in range(group):
            column = columns[:lanes, j : j + 1].astype(jnp.int32)
            hot.append(jnp.where(lane == column, 1.0, 0.0).astype(BF16))
        found = jnp.dot(jnp.concatenate(hot, axis=0), table[...], preferred_element_type=F32)
        found = found.astype(BF16)
        for j in range(group):
            k = kth(g * group + j)
            for user in range(users):
                start = j * lanes + user * slots
                ready[user, k] = found[start : start + slots]

            @pl.when(k != 0)
            def _():
                give(k).start()

    own = pltpu.make_async_copy(ready.at[:, 0], fetched.at[:, 0], self_sem)
    own.start()

    @pl.loop(1, count)
    def _(k):
        ask(k).wait_send()
        give(k).wait()

    own.wait()


def project_kernel(inner_dim, conv_dim, place, rows, gain, weight, item, gate, conv, step):
    count = rows.shape[0]
    lane = lax.broadcasted_iota(jnp.int32, (BLOCK, count), 1)
    hot = jnp.where(lane == place[...], 1.0, 0.0).astype(BF16)
    wide = jnp.dot(hot, rows[...], preferred_element_type=F32)
    item[...] = wide.astype(BF16)
    scale = lax.rsqrt(jnp.mean(wide * wide, axis=-1, keepdims=True) + 1e-05)
    normed = (wide * scale * gain[...]).astype(BF16)
    gate[...] = jnp.dot(normed, weight[:, :inner_dim], preferred_element_type=F32).astype(BF16)
    conv[...] = jnp.dot(
        normed, weight[:, inner_dim : inner_dim + conv_dim], preferred_element_type=F32
    ).astype(BF16)
    step[...] = (
        jnp.dot(normed, weight[:, inner_dim + conv_dim :], preferred_element_type=F32)
        .astype(BF16)
        .astype(F32)
    )


def state_kernel(
    inner_dim, conv, step, gap, alive, edge, taps, bias, dt_bias, rate,
    x_out, bc_out, cum_out, entering, before, final, factor,
    padded, running, gone,
):
    head_count = step.shape[1]
    state_dim = entering.shape[1]
    block_index = pl.program_id(1)

    @pl.when(block_index == 0)
    def _():
        padded[0:8] = edge[...].astype(F32)
        running[...] = jnp.zeros_like(running)
        gone[...] = jnp.zeros_like(gone)

    padded[8 : 8 + BLOCK] = conv[...].astype(F32)
    total = bias[...] + taps[0:1] * padded[5 : 5 + BLOCK]
    for k in range(1, 4):
        total = total + taps[k : k + 1] * padded[5 + k : 5 + k + BLOCK]
    padded[0:8] = padded[BLOCK : BLOCK + 8]
    out = silu(total).astype(BF16)
    x = out[:, :inner_dim]
    bc = out[:, inner_dim:]
    bc_out[...] = bc
    raw = step[...] + dt_bias[...]
    soft = jnp.maximum(raw, 0.0) + jnp.log1p(jnp.exp(-jnp.abs(raw)))
    steps = alive[...] * soft
    log_decay = -rate[...] * gap[...] * steps
    below = lax.broadcasted_iota(jnp.int32, (BLOCK, BLOCK), 0) >= lax.broadcasted_iota(
        jnp.int32, (BLOCK, BLOCK), 1
    )
    cum = jnp.dot(
        jnp.where(below, 1.0, 0.0), log_decay, preferred_element_type=F32,
        precision=lax.Precision.HIGHEST,
    )
    cum_out[...] = cum
    last = cum[BLOCK - 1 : BLOCK]
    spread = head_spread(head_count, inner_dim)
    x_out[...] = (over_channels(steps, spread) * x.astype(F32)).astype(BF16)
    scaled = (over_channels(jnp.exp(last - cum) * steps, spread) * x.astype(F32)).astype(BF16)
    block_state = lax.dot_general(
        bc[:, :state_dim], scaled, (((0,), (0,)), ((), ())), preferred_element_type=F32
    )
    entering[0] = running[...]
    before[0] = over_channels(jnp.exp(gone[...]), spread)
    fade = over_channels(jnp.broadcast_to(jnp.exp(last), gone.shape), spread)
    new = fade[0:1] * running[...] + block_state
    running[...] = new
    gone[...] = gone[...] + last
    final[...] = new
    factor[...] = over_channels(jnp.exp(gone[...]), spread)


def local_kernel(
    head_count, xs, bc, cum, state, factor,
    y, incoming, scores, across, inbox, outbox, send_sem, recv_sem,
):
    length, here = (lax.axis_size("tm"), lax.axis_index("tm"))
    users, events, inner_dim = xs.shape
    state_dim = bc.shape[2] // 2
    blocks = events // BLOCK
    width = 2 * (inner_dim // head_count)
    pairs = head_count // 2
    chunks = users * pairs
    delay = 2

    barrier = pltpu.get_barrier_semaphore()

    @pl.when(here > 0)
    def _():
        pl.semaphore_signal(
            barrier, inc=1, device_id=(jnp.maximum(here - 1, 0), lax.axis_index("table")),
            device_id_type=pl.DeviceIdType.MESH,
        )

    @pl.when(here < length - 1)
    def _():
        pl.semaphore_signal(
            barrier, inc=1,
            device_id=(jnp.minimum(here + 1, length - 1), lax.axis_index("table")),
            device_id_type=pl.DeviceIdType.MESH,
        )

    pl.semaphore_wait(barrier, jnp.minimum(here, 1) + jnp.minimum(length - 1 - here, 1))

    def onward(c):
        return pltpu.make_async_remote_copy(
            src_ref=outbox.at[c],
            dst_ref=inbox.at[c],
            send_sem=send_sem.at[c],
            recv_sem=recv_sem.at[c],
            device_id=(jnp.minimum(here + 1, length - 1), lax.axis_index("table")),
            device_id_type=pl.DeviceIdType.MESH,
        )

    def pass_chunk(c):
        user = c % users
        lanes = pl.ds(pl.multiple_of((c // users) * width, width), width)

        @pl.when(here == 0)
        def _():
            incoming[user, :, lanes] = jnp.zeros((state_dim, width), F32)

        @pl.when(here > 0)
        def _():
            onward(c).wait_recv()
            incoming[user, :, lanes] = inbox[c].astype(F32)

        @pl.when(here < length - 1)
        def _():
            after = factor[user, 0:1, lanes] * incoming[user, :, lanes] + state[user, :, lanes]
            outbox[c] = after.astype(BF16)
            onward(c).start()

    def slot(t):
        c = t - delay * here

        @pl.when((c >= 0) & (c < chunks))
        def _():
            pass_chunk(c)

    below = lax.broadcasted_iota(jnp.int32, (BLOCK, BLOCK), 0) >= lax.broadcasted_iota(
        jnp.int32, (BLOCK, BLOCK), 1
    )

    @pl.loop(0, users * blocks)
    def _(r):
        rows = pl.ds(pl.multiple_of((r % blocks) * BLOCK, BLOCK), BLOCK)
        both = bc[r // blocks, rows, :]
        found = lax.dot_general(
            both[:, state_dim:], both[:, :state_dim], (((1,), (1,)), ((), ())),
            preferred_element_type=F32,
        )
        scores[r] = jnp.where(below, found, 0.0)
        across[r] = cum[r // blocks, rows, :].T

    left = lax.broadcasted_iota(jnp.int32, (BLOCK, width), 1) < width // 2
    for pair in range(pairs):
        lanes = slice(pair * width, (pair + 1) * width)

        @pl.loop(0, users * blocks)
        def _(r, pair=pair, lanes=lanes):
            user = r // blocks

            @pl.when(r % blocks == 0)
            def _():
                slot(pair * users + user)

            rows = pl.ds(pl.multiple_of((r % blocks) * BLOCK, BLOCK), BLOCK)
            values = xs[user, rows, lanes]
            parts = []
            for h in (2 * pair, 2 * pair + 1):
                down = cum[user, rows, h : h + 1]
                fading = jnp.exp(jnp.minimum(down - across[r, h : h + 1, :], 0.0))
                mixing = (scores[r] * fading).astype(BF16)
                parts.append(jnp.dot(mixing, values, preferred_element_type=F32))
            y[user, rows, lanes] = jnp.where(left, parts[0], parts[1]).astype(BF16)

    @pl.loop(chunks, chunks + delay * (length - 1))
    def _(t):
        slot(t)

    @pl.when(here < length - 1)
    def _():
        @pl.loop(0, chunks)
        def _(c):
            onward(c).wait_send()


def emit_kernel(
    y, bc, cum, gate, item, alive, entering, before, incoming, gain, weight, out
):
    head_count = cum.shape[1]
    inner_dim = y.shape[1]
    state_dim = bc.shape[1] // 2
    spread = head_spread(head_count, inner_dim)
    held = (entering[0] + before[0, 0:1] * incoming[...]).astype(BF16)
    carried = jnp.dot(bc[:, state_dim:], held, preferred_element_type=F32)
    response = y[...].astype(F32) + over_channels(jnp.exp(cum[...]), spread) * carried
    gated = response * silu(gate[...].astype(F32))
    squares = lax.dot_general(
        (gated * gated).astype(BF16), spread, (((1,), (1,)), ((), ())),
        preferred_element_type=F32,
    )
    scale = lax.rsqrt(squares * (head_count / inner_dim) + 1e-05)
    normed = (gated * over_channels(scale, spread) * gain[...]).astype(BF16)
    mixed = jnp.dot(normed, weight[...], preferred_element_type=F32)
    out[...] = (alive[...] * (item[...].astype(F32) + mixed)).astype(BF16)


def rows_of(width):
    return pl.BlockSpec((None, BLOCK, width), lambda u, i: (u, i, 0))


def whole(*shape):
    return pl.BlockSpec(shape, lambda u, i: (0,) * len(shape))


def user_of(*shape):
    return pl.BlockSpec((None, *shape), lambda u, i: (u,) + (0,) * len(shape))


def one_of(*shape):
    return pl.BlockSpec((None, 1, *shape), lambda u, i: (u, i) + (0,) * len(shape))


def params():
    return pltpu.CompilerParams(
        vmem_limit_bytes=VMEM_LIMIT, dimension_semantics=("arbitrary", "arbitrary")
    )


def cost(flops, size, exps=0):
    return pl.CostEstimate(flops=flops, bytes_accessed=size, transcendentals=exps)


def struct(shape, dtype):
    return jax.ShapeDtypeStruct(shape, dtype)


def per_device(
    item_owner,
    item_row,
    history_len,
    event_gap,
    item_table,
    norm_gain,
    in_weight,
    conv_weight,
    conv_bias,
    dt_bias,
    decay_rate,
    out_gain,
    emitted_projection,
):
    user_count, events = item_row.shape
    model_dim = item_table.shape[1]
    head_count = dt_bias.shape[0]
    inner_dim = emitted_projection.shape[0]
    conv_dim = conv_weight.shape[1]
    state_dim = (conv_dim - inner_dim) // 2
    projected_dim = in_weight.shape[1]
    devices = lax.axis_size("tm") * lax.axis_size("table")
    capacity = max(2 * events // devices, 2)
    blocks = events // BLOCK

    owners = item_owner[..., 0]
    owner_match = owners[..., None] == jnp.arange(devices, dtype=jnp.int32)
    owner_hot = owner_match.astype(BF16)
    earlier_mask = (jnp.arange(events)[:, None] > jnp.arange(events)[None, :]).astype(BF16)
    earlier_counts = jnp.einsum(
        "ts,usd->utd", earlier_mask, owner_hot, preferred_element_type=F32
    )
    slots = jnp.sum(jnp.where(owner_match, earlier_counts, 0.0), axis=-1).astype(jnp.int32)
    slot_match = slots[..., None] == jnp.arange(capacity, dtype=jnp.int32)
    row_high = item_row // 64
    row_low = item_row - row_high * 64
    parts = jnp.concatenate(
        [
            jnp.where(slot_match, row_high[..., None], 0),
            jnp.where(slot_match, row_low[..., None], 0),
        ],
        axis=-1,
    ).astype(BF16)
    asked = jnp.einsum("utd,utc->duc", owner_hot, parts, preferred_element_type=F32)
    requests = (64.0 * asked[..., :capacity] + asked[..., capacity:]).astype(jnp.int32)
    slot_rows = -(-capacity // 16) * 16
    slots_all = devices * slot_rows
    requests = jnp.pad(requests, ((0, 0), (0, 0), (0, slot_rows - capacity)))
    requests = requests.reshape(devices, 1, user_count * slot_rows)
    lanes = -(-user_count * slot_rows // 128) * 128
    requests = jnp.pad(requests, ((0, 0), (0, 0), (0, lanes - user_count * slot_rows)))
    here = lax.axis_index("tm") * lax.axis_size("table") + lax.axis_index("table")
    place = ((owners - here) % devices) * slot_rows + slots
    group = 4
    buffer = (user_count, devices, slot_rows, model_dim)
    fetched = pl.pallas_call(
        lambda *refs: exchange_kernel(devices, group, *refs),
        in_specs=[pl.BlockSpec(memory_space=pltpu.VMEM), pl.BlockSpec(memory_space=pl.ANY)],
        out_specs=pl.BlockSpec(memory_space=pl.ANY),
        out_shape=struct(buffer, BF16),
        scratch_shapes=[
            pltpu.VMEM(item_table.shape, BF16),
            pltpu.VMEM((8, lanes), F32),
            pltpu.VMEM((devices, 1, lanes), jnp.int32),
            pltpu.VMEM(buffer, BF16),
            pltpu.SemaphoreType.DMA,
            pltpu.SemaphoreType.DMA,
            pltpu.SemaphoreType.DMA((devices,)),
            pltpu.SemaphoreType.DMA((devices,)),
            pltpu.SemaphoreType.DMA((devices,)),
            pltpu.SemaphoreType.DMA((devices,)),
        ],
        compiler_params=pltpu.CompilerParams(
            vmem_limit_bytes=VMEM_LIMIT, collective_id=0, has_side_effects=True
        ),
        cost_estimate=cost(13 << 30, 10 << 20),
        name="exchange",
    )(requests, item_table).reshape(user_count, slots_all, model_dim)

    positions = lax.axis_index("tm") * events + jnp.arange(events, dtype=jnp.int32)
    alive = (positions[None, :] < history_len[:, None]).astype(F32)

    alive_column = alive[..., None]
    item, gate, conv, step = pl.pallas_call(
        lambda *refs: project_kernel(inner_dim, conv_dim, *refs),
        grid=(user_count, blocks),
        in_specs=[
            rows_of(1),
            user_of(slots_all, model_dim),
            whole(1, model_dim),
            whole(model_dim, projected_dim),
        ],
        out_specs=[rows_of(model_dim), rows_of(inner_dim), rows_of(conv_dim), rows_of(head_count)],
        out_shape=[
            struct((user_count, events, model_dim), BF16),
            struct((user_count, events, inner_dim), BF16),
            struct((user_count, events, conv_dim), BF16),
            struct((user_count, events, head_count), F32),
        ],
        compiler_params=params(),
        cost_estimate=cost(2 * events * model_dim * (projected_dim + slots_all), 9 << 20),
        name="project",
    )(place[..., None], fetched, norm_gain[None], in_weight)
    edge = passed_along(conv[:, events - 8 :], "tm", 1)
    xs, bc, cum, entering, before, final, factor = pl.pallas_call(
        lambda *refs: state_kernel(inner_dim, *refs),
        grid=(user_count, blocks),
        in_specs=[
            rows_of(conv_dim),
            rows_of(head_count),
            rows_of(1),
            rows_of(1),
            user_of(8, conv_dim),
            whole(4, conv_dim),
            whole(1, conv_dim),
            whole(1, head_count),
            whole(1, head_count),
        ],
        out_specs=[
            rows_of(inner_dim),
            rows_of(2 * state_dim),
            rows_of(head_count),
            one_of(state_dim, inner_dim),
            one_of(8, inner_dim),
            user_of(state_dim, inner_dim),
            user_of(8, inner_dim),
        ],
        out_shape=[
            struct((user_count, events, inner_dim), BF16),
            struct((user_count, events, 2 * state_dim), BF16),
            struct((user_count, events, head_count), F32),
            struct((user_count, blocks, state_dim, inner_dim), F32),
            struct((user_count, blocks, 8, inner_dim), F32),
            struct((user_count, state_dim, inner_dim), F32),
            struct((user_count, 8, inner_dim), F32),
        ],
        scratch_shapes=[
            pltpu.VMEM((BLOCK + 8, conv_dim), F32),
            pltpu.VMEM((state_dim, inner_dim), F32),
            pltpu.VMEM((8, head_count), F32),
        ],
        compiler_params=params(),
        cost_estimate=cost(4 << 30, 8 << 20, events * conv_dim),
        name="states",
    )(
        conv, step, event_gap[..., None], alive_column, edge,
        conv_weight, conv_bias[None], dt_bias[None], decay_rate[None],
    )
    chunks = user_count * (head_count // 2)
    pair_width = 2 * (inner_dim // head_count)
    y, incoming = pl.pallas_call(
        lambda *refs: local_kernel(head_count, *refs),
        in_specs=[pl.BlockSpec(memory_space=pltpu.VMEM)] * 5,
        out_specs=[pl.BlockSpec(memory_space=pltpu.VMEM)] * 2,
        out_shape=[
            struct((user_count, events, inner_dim), BF16),
            struct((user_count, state_dim, inner_dim), F32),
        ],
        scratch_shapes=[
            pltpu.VMEM((user_count * blocks, BLOCK, BLOCK), F32),
            pltpu.VMEM((user_count * blocks, head_count, BLOCK), F32),
            pltpu.VMEM((chunks, state_dim, pair_width), BF16),
            pltpu.VMEM((chunks, state_dim, pair_width), BF16),
            pltpu.SemaphoreType.DMA((chunks,)),
            pltpu.SemaphoreType.DMA((chunks,)),
        ],
        compiler_params=pltpu.CompilerParams(
            vmem_limit_bytes=VMEM_LIMIT, collective_id=1, has_side_effects=True
        ),
        cost_estimate=cost(8 << 30, 8 << 20, user_count * events * BLOCK * head_count),
        name="local",
    )(xs, bc, cum, final, factor)
    return (
        pl.pallas_call(
            emit_kernel,
            grid=(user_count, blocks),
            in_specs=[
                rows_of(inner_dim),
                rows_of(2 * state_dim),
                rows_of(head_count),
                rows_of(inner_dim),
                rows_of(model_dim),
                rows_of(1),
                one_of(state_dim, inner_dim),
                one_of(8, inner_dim),
                user_of(state_dim, inner_dim),
                whole(1, inner_dim),
                whole(inner_dim, model_dim),
            ],
            out_specs=rows_of(model_dim),
            out_shape=struct((user_count, events, model_dim), BF16),
            compiler_params=params(),
            cost_estimate=cost(4 << 30, 9 << 20, events * inner_dim),
            name="emit",
        )(
            y, bc, cum, gate, item, alive_column, entering, before, incoming,
            out_gain[None], emitted_projection,
        )
    )


def solution(mesh):
    in_specs = (
        P("table", "tm", None),
        P("table", "tm"),
        P("table"),
        P("table", "tm"),
        P(("tm", "table"), None),
        P(),
        P(),
        P(),
        P(),
        P(),
        P(),
        P(),
        P(),
    )
    out_specs = P("table", "tm", None)
    return jax.shard_map(
        per_device, mesh=mesh, in_specs=in_specs, out_specs=out_specs, check_vma=False
    )
```

```python
import jax
import jax.numpy as jnp
from jax import lax
from jax.experimental import pallas as pl
from jax.experimental.pallas import tpu as pltpu
from jax.sharding import PartitionSpec as P

BLOCK = 256
F32 = jnp.float32
BF16 = jnp.bfloat16
VMEM_LIMIT = 40 * 1024 * 1024


def passed_along(block, axis, distance):
    devices = range(lax.axis_size(axis))
    route = [(i - distance, i) for i in devices if i - distance in devices]
    return lax.ppermute(block, axis, route)


def head_spread(head_count, inner_dim):
    head_dim = inner_dim // head_count
    lane = lax.broadcasted_iota(jnp.int32, (head_count, inner_dim), 1)
    row = lax.broadcasted_iota(jnp.int32, (head_count, inner_dim), 0)
    first = row * head_dim
    return jnp.where((lane >= first) & (lane < first + head_dim), 1.0, 0.0).astype(BF16)


def over_channels(values, spread):
    high = values.astype(BF16)
    low = (values - high.astype(F32)).astype(BF16)
    return jnp.dot(high, spread, preferred_element_type=F32) + jnp.dot(
        low, spread, preferred_element_type=F32
    )


def silu(v):
    return v / (1.0 + jnp.exp(-v))


def exchange_kernel(
    count, group, requests, table_hbm, fetched,
    table, asked, wanted, ready, table_sem, self_sem, ask_send, ask_recv, row_send, row_recv,
):
    tm, across = (lax.axis_index("tm"), lax.axis_index("table"))
    width = lax.axis_size("table")
    me = tm * width + across
    half = count // 2

    def device(index):
        return (index // width, index % width)

    def ask(k):
        target = (me + k) % count
        return pltpu.make_async_remote_copy(
            src_ref=requests.at[target],
            dst_ref=wanted.at[k],
            send_sem=ask_send.at[k],
            recv_sem=ask_recv.at[k],
            device_id=device(target),
            device_id_type=pl.DeviceIdType.MESH,
        )

    def give(k):
        return pltpu.make_async_remote_copy(
            src_ref=ready.at[:, k],
            dst_ref=fetched.at[:, k],
            send_sem=row_send.at[k],
            recv_sem=row_recv.at[k],
            device_id=device((me + count - k) % count),
            device_id_type=pl.DeviceIdType.MESH,
        )

    asked[...] = jnp.zeros_like(asked)
    loading = pltpu.make_async_copy(table_hbm, table, table_sem)
    loading.start()
    own_ask = pltpu.make_async_copy(requests.at[me], wanted.at[0], self_sem)
    own_ask.start()
    barrier = pltpu.get_barrier_semaphore()

    @pl.loop(1, count)
    def _(k):
        pl.semaphore_signal(
            barrier, inc=1, device_id=device((me + k) % count),
            device_id_type=pl.DeviceIdType.MESH,
        )

    pl.semaphore_wait(barrier, count - 1)

    def kth(p):
        return jnp.where(p % 2 == 0, half + p // 2, ((p + 1) // 2) % half)

    @pl.loop(0, count - 1)
    def _(p):
        ask(kth(p)).start()

    own_ask.wait()
    loading.wait()
    users, _, slots, _ = ready.shape
    lanes = users * slots
    rows = table.shape[0]

    @pl.loop(0, count // group)
    def _(g):
        for j in range(group):
            k = kth(g * group + j)

            @pl.when(k != 0)
            def _():
                ask(k).wait_recv()

            asked[j : j + 1] = wanted[k].astype(F32)
        columns = asked[...].T
        hot = []
        lane = lax.broadcasted_iota(jnp.int32, (lanes, rows), 1)
        for j in range(group):
            column = columns[:lanes, j : j + 1].astype(jnp.int32)
            hot.append(jnp.where(lane == column, 1.0, 0.0).astype(BF16))
        found = jnp.dot(jnp.concatenate(hot, axis=0), table[...], preferred_element_type=F32)
        found = found.astype(BF16)
        for j in range(group):
            k = kth(g * group + j)
            for user in range(users):
                start = j * lanes + user * slots
                ready[user, k] = found[start : start + slots]

            @pl.when(k != 0)
            def _():
                give(k).start()

    own = pltpu.make_async_copy(ready.at[:, 0], fetched.at[:, 0], self_sem)
    own.start()

    @pl.loop(1, count)
    def _(k):
        ask(k).wait_send()
        give(k).wait()

    own.wait()


def project_kernel(inner_dim, conv_dim, place, rows, gain, weight, item, gate, conv, step):
    count = rows.shape[0]
    lane = lax.broadcasted_iota(jnp.int32, (BLOCK, count), 1)
    hot = jnp.where(lane == place[...], 1.0, 0.0).astype(BF16)
    wide = jnp.dot(hot, rows[...], preferred_element_type=F32)
    item[...] = wide.astype(BF16)
    scale = lax.rsqrt(jnp.mean(wide * wide, axis=-1, keepdims=True) + 1e-05)
    normed = (wide * scale * gain[...]).astype(BF16)
    gate[...] = jnp.dot(normed, weight[:, :inner_dim], preferred_element_type=F32).astype(BF16)
    conv[...] = jnp.dot(
        normed, weight[:, inner_dim : inner_dim + conv_dim], preferred_element_type=F32
    ).astype(BF16)
    step[...] = (
        jnp.dot(normed, weight[:, inner_dim + conv_dim :], preferred_element_type=F32)
        .astype(BF16)
        .astype(F32)
    )


def state_kernel(
    inner_dim, conv, step, gap, alive, edge, taps, bias, dt_bias, rate,
    x_out, bc_out, cum_out, entering, before, final, factor,
    padded, running, gone,
):
    head_count = step.shape[1]
    state_dim = entering.shape[1]
    block_index = pl.program_id(1)

    @pl.when(block_index == 0)
    def _():
        padded[0:8] = edge[...].astype(F32)
        running[...] = jnp.zeros_like(running)
        gone[...] = jnp.zeros_like(gone)

    padded[8 : 8 + BLOCK] = conv[...].astype(F32)
    total = bias[...] + taps[0:1] * padded[5 : 5 + BLOCK]
    for k in range(1, 4):
        total = total + taps[k : k + 1] * padded[5 + k : 5 + k + BLOCK]
    padded[0:8] = padded[BLOCK : BLOCK + 8]
    out = silu(total).astype(BF16)
    x = out[:, :inner_dim]
    bc = out[:, inner_dim:]
    bc_out[...] = bc
    raw = step[...] + dt_bias[...]
    soft = jnp.maximum(raw, 0.0) + jnp.log1p(jnp.exp(-jnp.abs(raw)))
    steps = alive[...] * soft
    log_decay = -rate[...] * gap[...] * steps
    below = lax.broadcasted_iota(jnp.int32, (BLOCK, BLOCK), 0) >= lax.broadcasted_iota(
        jnp.int32, (BLOCK, BLOCK), 1
    )
    cum = jnp.dot(
        jnp.where(below, 1.0, 0.0), log_decay, preferred_element_type=F32,
        precision=lax.Precision.HIGHEST,
    )
    cum_out[...] = cum
    last = cum[BLOCK - 1 : BLOCK]
    spread = head_spread(head_count, inner_dim)
    x_out[...] = (over_channels(steps, spread) * x.astype(F32)).astype(BF16)
    scaled = (over_channels(jnp.exp(last - cum) * steps, spread) * x.astype(F32)).astype(BF16)
    block_state = lax.dot_general(
        bc[:, :state_dim], scaled, (((0,), (0,)), ((), ())), preferred_element_type=F32
    )
    entering[0] = running[...]
    before[0] = over_channels(jnp.exp(gone[...]), spread)
    fade = over_channels(jnp.broadcast_to(jnp.exp(last), gone.shape), spread)
    new = fade[0:1] * running[...] + block_state
    running[...] = new
    gone[...] = gone[...] + last
    final[...] = new
    factor[...] = over_channels(jnp.exp(gone[...]), spread)


def local_kernel(
    head_count, xs, bc, cum, state, factor,
    y, incoming, scores, across, inbox, outbox, send_sem, recv_sem,
):
    length, here = (lax.axis_size("tm"), lax.axis_index("tm"))
    users, events, inner_dim = xs.shape
    state_dim = bc.shape[2] // 2
    blocks = events // BLOCK
    width = 2 * (inner_dim // head_count)
    pairs = head_count // 2
    chunks = users * pairs
    delay = 4

    barrier = pltpu.get_barrier_semaphore()

    @pl.when(here > 0)
    def _():
        pl.semaphore_signal(
            barrier, inc=1, device_id=(jnp.maximum(here - 1, 0), lax.axis_index("table")),
            device_id_type=pl.DeviceIdType.MESH,
        )

    @pl.when(here < length - 1)
    def _():
        pl.semaphore_signal(
            barrier, inc=1,
            device_id=(jnp.minimum(here + 1, length - 1), lax.axis_index("table")),
            device_id_type=pl.DeviceIdType.MESH,
        )

    pl.semaphore_wait(barrier, jnp.minimum(here, 1) + jnp.minimum(length - 1 - here, 1))

    def onward(c):
        return pltpu.make_async_remote_copy(
            src_ref=outbox.at[c],
            dst_ref=inbox.at[c],
            send_sem=send_sem.at[c],
            recv_sem=recv_sem.at[c],
            device_id=(jnp.minimum(here + 1, length - 1), lax.axis_index("table")),
            device_id_type=pl.DeviceIdType.MESH,
        )

    def pass_chunk(c):
        user = c % users
        lanes = pl.ds(pl.multiple_of((c // users) * width, width), width)

        @pl.when(here == 0)
        def _():
            incoming[user, :, lanes] = jnp.zeros((state_dim, width), F32)

        @pl.when(here > 0)
        def _():
            onward(c).wait_recv()
            incoming[user, :, lanes] = inbox[c].astype(F32)

        @pl.when(here < length - 1)
        def _():
            after = factor[user, 0:1, lanes] * incoming[user, :, lanes] + state[user, :, lanes]
            outbox[c] = after.astype(BF16)
            onward(c).start()

    def slot(t):
        c = t - delay * here

        @pl.when((c >= 0) & (c < chunks))
        def _():
            pass_chunk(c)

    below = lax.broadcasted_iota(jnp.int32, (BLOCK, BLOCK), 0) >= lax.broadcasted_iota(
        jnp.int32, (BLOCK, BLOCK), 1
    )

    @pl.loop(0, users * blocks)
    def _(r):
        rows = pl.ds(pl.multiple_of((r % blocks) * BLOCK, BLOCK), BLOCK)
        both = bc[r // blocks, rows, :]
        found = lax.dot_general(
            both[:, state_dim:], both[:, :state_dim], (((1,), (1,)), ((), ())),
            preferred_element_type=F32,
        )
        scores[r] = jnp.where(below, found, 0.0)
        across[r] = cum[r // blocks, rows, :].T

    left = lax.broadcasted_iota(jnp.int32, (BLOCK, width), 1) < width // 2
    for pair in range(pairs):
        lanes = slice(pair * width, (pair + 1) * width)

        @pl.loop(0, users * blocks)
        def _(r, pair=pair, lanes=lanes):
            user = r // blocks

            slot(pair * users * blocks + r)

            rows = pl.ds(pl.multiple_of((r % blocks) * BLOCK, BLOCK), BLOCK)
            values = xs[user, rows, lanes]
            parts = []
            for h in (2 * pair, 2 * pair + 1):
                down = cum[user, rows, h : h + 1]
                fading = jnp.exp(jnp.minimum(down - across[r, h : h + 1, :], 0.0))
                mixing = (scores[r] * fading).astype(BF16)
                parts.append(jnp.dot(mixing, values, preferred_element_type=F32))
            y[user, rows, lanes] = jnp.where(left, parts[0], parts[1]).astype(BF16)

    done = pairs * users * blocks
    last = chunks + delay * (length - 1)
    if last > done:

        @pl.loop(done, last)
        def _(t):
            slot(t)

    @pl.when(here < length - 1)
    def _():
        @pl.loop(0, chunks)
        def _(c):
            onward(c).wait_send()


def emit_kernel(
    y, bc, cum, gate, item, alive, entering, before, incoming, gain, weight, out
):
    head_count = cum.shape[1]
    inner_dim = y.shape[1]
    state_dim = bc.shape[1] // 2
    spread = head_spread(head_count, inner_dim)
    held = (entering[0] + before[0, 0:1] * incoming[...]).astype(BF16)
    carried = jnp.dot(bc[:, state_dim:], held, preferred_element_type=F32)
    response = y[...].astype(F32) + over_channels(jnp.exp(cum[...]), spread) * carried
    gated = response * silu(gate[...].astype(F32))
    squares = lax.dot_general(
        (gated * gated).astype(BF16), spread, (((1,), (1,)), ((), ())),
        preferred_element_type=F32,
    )
    scale = lax.rsqrt(squares * (head_count / inner_dim) + 1e-05)
    normed = (gated * over_channels(scale, spread) * gain[...]).astype(BF16)
    mixed = jnp.dot(normed, weight[...], preferred_element_type=F32)
    out[...] = (alive[...] * (item[...].astype(F32) + mixed)).astype(BF16)


def rows_of(width):
    return pl.BlockSpec((None, BLOCK, width), lambda u, i: (u, i, 0))


def whole(*shape):
    return pl.BlockSpec(shape, lambda u, i: (0,) * len(shape))


def user_of(*shape):
    return pl.BlockSpec((None, *shape), lambda u, i: (u,) + (0,) * len(shape))


def one_of(*shape):
    return pl.BlockSpec((None, 1, *shape), lambda u, i: (u, i) + (0,) * len(shape))


def params():
    return pltpu.CompilerParams(
        vmem_limit_bytes=VMEM_LIMIT, dimension_semantics=("arbitrary", "arbitrary")
    )


def cost(flops, size, exps=0):
    return pl.CostEstimate(flops=flops, bytes_accessed=size, transcendentals=exps)


def struct(shape, dtype):
    return jax.ShapeDtypeStruct(shape, dtype)


def per_device(
    item_owner,
    item_row,
    history_len,
    event_gap,
    item_table,
    norm_gain,
    in_weight,
    conv_weight,
    conv_bias,
    dt_bias,
    decay_rate,
    out_gain,
    emitted_projection,
):
    user_count, events = item_row.shape
    model_dim = item_table.shape[1]
    head_count = dt_bias.shape[0]
    inner_dim = emitted_projection.shape[0]
    conv_dim = conv_weight.shape[1]
    state_dim = (conv_dim - inner_dim) // 2
    projected_dim = in_weight.shape[1]
    devices = lax.axis_size("tm") * lax.axis_size("table")
    capacity = max(2 * events // devices, 2)
    blocks = events // BLOCK

    owners = item_owner[..., 0]
    owner_match = owners[..., None] == jnp.arange(devices, dtype=jnp.int32)
    owner_hot = owner_match.astype(BF16)
    earlier_mask = (jnp.arange(events)[:, None] > jnp.arange(events)[None, :]).astype(BF16)
    earlier_counts = jnp.einsum(
        "ts,usd->utd", earlier_mask, owner_hot, preferred_element_type=F32
    )
    slots = jnp.sum(jnp.where(owner_match, earlier_counts, 0.0), axis=-1).astype(jnp.int32)
    slot_match = slots[..., None] == jnp.arange(capacity, dtype=jnp.int32)
    row_high = item_row // 64
    row_low = item_row - row_high * 64
    parts = jnp.concatenate(
        [
            jnp.where(slot_match, row_high[..., None], 0),
            jnp.where(slot_match, row_low[..., None], 0),
        ],
        axis=-1,
    ).astype(BF16)
    asked = jnp.einsum("utd,utc->duc", owner_hot, parts, preferred_element_type=F32)
    requests = (64.0 * asked[..., :capacity] + asked[..., capacity:]).astype(jnp.int32)
    slot_rows = -(-capacity // 16) * 16
    slots_all = devices * slot_rows
    requests = jnp.pad(requests, ((0, 0), (0, 0), (0, slot_rows - capacity)))
    requests = requests.reshape(devices, 1, user_count * slot_rows)
    lanes = -(-user_count * slot_rows // 128) * 128
    requests = jnp.pad(requests, ((0, 0), (0, 0), (0, lanes - user_count * slot_rows)))
    here = lax.axis_index("tm") * lax.axis_size("table") + lax.axis_index("table")
    place = ((owners - here) % devices) * slot_rows + slots
    group = 4
    buffer = (user_count, devices, slot_rows, model_dim)
    fetched = pl.pallas_call(
        lambda *refs: exchange_kernel(devices, group, *refs),
        in_specs=[pl.BlockSpec(memory_space=pltpu.VMEM), pl.BlockSpec(memory_space=pl.ANY)],
        out_specs=pl.BlockSpec(memory_space=pl.ANY),
        out_shape=struct(buffer, BF16),
        scratch_shapes=[
            pltpu.VMEM(item_table.shape, BF16),
            pltpu.VMEM((8, lanes), F32),
            pltpu.VMEM((devices, 1, lanes), jnp.int32),
            pltpu.VMEM(buffer, BF16),
            pltpu.SemaphoreType.DMA,
            pltpu.SemaphoreType.DMA,
            pltpu.SemaphoreType.DMA((devices,)),
            pltpu.SemaphoreType.DMA((devices,)),
            pltpu.SemaphoreType.DMA((devices,)),
            pltpu.SemaphoreType.DMA((devices,)),
        ],
        compiler_params=pltpu.CompilerParams(
            vmem_limit_bytes=VMEM_LIMIT, collective_id=0, has_side_effects=True
        ),
        cost_estimate=cost(13 << 30, 10 << 20),
        name="exchange",
    )(requests, item_table).reshape(user_count, slots_all, model_dim)

    positions = lax.axis_index("tm") * events + jnp.arange(events, dtype=jnp.int32)
    alive = (positions[None, :] < history_len[:, None]).astype(F32)

    alive_column = alive[..., None]
    item, gate, conv, step = pl.pallas_call(
        lambda *refs: project_kernel(inner_dim, conv_dim, *refs),
        grid=(user_count, blocks),
        in_specs=[
            rows_of(1),
            user_of(slots_all, model_dim),
            whole(1, model_dim),
            whole(model_dim, projected_dim),
        ],
        out_specs=[rows_of(model_dim), rows_of(inner_dim), rows_of(conv_dim), rows_of(head_count)],
        out_shape=[
            struct((user_count, events, model_dim), BF16),
            struct((user_count, events, inner_dim), BF16),
            struct((user_count, events, conv_dim), BF16),
            struct((user_count, events, head_count), F32),
        ],
        compiler_params=params(),
        cost_estimate=cost(2 * events * model_dim * (projected_dim + slots_all), 9 << 20),
        name="project",
    )(place[..., None], fetched, norm_gain[None], in_weight)
    edge = passed_along(conv[:, events - 8 :], "tm", 1)
    xs, bc, cum, entering, before, final, factor = pl.pallas_call(
        lambda *refs: state_kernel(inner_dim, *refs),
        grid=(user_count, blocks),
        in_specs=[
            rows_of(conv_dim),
            rows_of(head_count),
            rows_of(1),
            rows_of(1),
            user_of(8, conv_dim),
            whole(4, conv_dim),
            whole(1, conv_dim),
            whole(1, head_count),
            whole(1, head_count),
        ],
        out_specs=[
            rows_of(inner_dim),
            rows_of(2 * state_dim),
            rows_of(head_count),
            one_of(state_dim, inner_dim),
            one_of(8, inner_dim),
            user_of(state_dim, inner_dim),
            user_of(8, inner_dim),
        ],
        out_shape=[
            struct((user_count, events, inner_dim), BF16),
            struct((user_count, events, 2 * state_dim), BF16),
            struct((user_count, events, head_count), F32),
            struct((user_count, blocks, state_dim, inner_dim), F32),
            struct((user_count, blocks, 8, inner_dim), F32),
            struct((user_count, state_dim, inner_dim), F32),
            struct((user_count, 8, inner_dim), F32),
        ],
        scratch_shapes=[
            pltpu.VMEM((BLOCK + 8, conv_dim), F32),
            pltpu.VMEM((state_dim, inner_dim), F32),
            pltpu.VMEM((8, head_count), F32),
        ],
        compiler_params=params(),
        cost_estimate=cost(4 << 30, 8 << 20, events * conv_dim),
        name="states",
    )(
        conv, step, event_gap[..., None], alive_column, edge,
        conv_weight, conv_bias[None], dt_bias[None], decay_rate[None],
    )
    chunks = user_count * (head_count // 2)
    pair_width = 2 * (inner_dim // head_count)
    y, incoming = pl.pallas_call(
        lambda *refs: local_kernel(head_count, *refs),
        in_specs=[pl.BlockSpec(memory_space=pltpu.VMEM)] * 5,
        out_specs=[pl.BlockSpec(memory_space=pltpu.VMEM)] * 2,
        out_shape=[
            struct((user_count, events, inner_dim), BF16),
            struct((user_count, state_dim, inner_dim), F32),
        ],
        scratch_shapes=[
            pltpu.VMEM((user_count * blocks, BLOCK, BLOCK), F32),
            pltpu.VMEM((user_count * blocks, head_count, BLOCK), F32),
            pltpu.VMEM((chunks, state_dim, pair_width), BF16),
            pltpu.VMEM((chunks, state_dim, pair_width), BF16),
            pltpu.SemaphoreType.DMA((chunks,)),
            pltpu.SemaphoreType.DMA((chunks,)),
        ],
        compiler_params=pltpu.CompilerParams(
            vmem_limit_bytes=VMEM_LIMIT, collective_id=1, has_side_effects=True
        ),
        cost_estimate=cost(8 << 30, 8 << 20, user_count * events * BLOCK * head_count),
        name="local",
    )(xs, bc, cum, final, factor)
    return (
        pl.pallas_call(
            emit_kernel,
            grid=(user_count, blocks),
            in_specs=[
                rows_of(inner_dim),
                rows_of(2 * state_dim),
                rows_of(head_count),
                rows_of(inner_dim),
                rows_of(model_dim),
                rows_of(1),
                one_of(state_dim, inner_dim),
                one_of(8, inner_dim),
                user_of(state_dim, inner_dim),
                whole(1, inner_dim),
                whole(inner_dim, model_dim),
            ],
            out_specs=rows_of(model_dim),
            out_shape=struct((user_count, events, model_dim), BF16),
            compiler_params=params(),
            cost_estimate=cost(4 << 30, 9 << 20, events * inner_dim),
            name="emit",
        )(
            y, bc, cum, gate, item, alive_column, entering, before, incoming,
            out_gain[None], emitted_projection,
        )
    )


def solution(mesh):
    in_specs = (
        P("table", "tm", None),
        P("table", "tm"),
        P("table"),
        P("table", "tm"),
        P(("tm", "table"), None),
        P(),
        P(),
        P(),
        P(),
        P(),
        P(),
        P(),
        P(),
    )
    out_specs = P("table", "tm", None)
    return jax.shard_map(
        per_device, mesh=mesh, in_specs=in_specs, out_specs=out_specs, check_vma=False
    )
```
